512 devices in a mesh: rep: 16 (over z, y_lo), tp: 8 (over x, core), fsdp: 4 (over y_hi).
Axes of the slice: x: 4, y: 8 (y_hi: 4, y_lo: 2; y = y_hi * 2 + y_lo), z: 8, core: 2. Of those that a mesh axis runs over, the one named last changes fastest.
Arguments:
- hidden_in: bfloat16 [32, 2, 5120], P('rep'), may hold values from -6 to 6
- frozen_query_matrix: bfloat16 [5120, 8192], P(None, ('tp', 'fsdp')), may hold values from -0.078125 to 0.078125
- factor_down: bfloat16 [5120, 64], P('rep'), may hold values from -0.078125 to 0.078125
- factor_up: bfloat16 [64, 8192], P('rep', ('tp', 'fsdp')), may hold values from -0.75 to 0.75
- query_gain: float32 [128], replicated, may hold values from 0.1 to 1.9
- key_cache: bfloat16 [32, 4096, 1024], P('rep', 'fsdp', 'tp'), may hold values from -1600 to 1600
- value_cache: bfloat16 [32, 4096, 1024], P('rep', 'fsdp', 'tp'), may hold values from -6 to 6
- new_keys: bfloat16 [32, 2, 1024], P('rep', None, 'tp'), may hold values from -15 to 15
- new_values: bfloat16 [32, 2, 1024], P('rep', None, 'tp'), may hold values from -6 to 6
- cache_lengths: int32 [32], P('rep'), may hold values from 1024 to 4096, as said below
Outputs:
- attended: bfloat16 [32, 2, 8192], P('rep', None, ('tp', 'fsdp'))
The draws below stay inside these ranges and needn't reach their ends.
Inputs may be any that keep to these rules, and one draw needn't show every extreme that they name: `cache_lengths`: some row has exactly 4096 valid slots.
All inputs are finite; a program needn't handle non-finite values.
Results may differ from the reference program's by a relative error of at most 0.029.
Values may be sent and summed in bfloat16 or wider, within the bound.
No kernel may reach another device: no remote copies, remote signals or barrier semaphores. Data moves between devices by JAX's collectives and lax.ppermute only.
A program may use at most 64 MiB of HBM per device.

```python
import jax
import jax.numpy as jnp
from jax import lax

D = 5120
QUERY_HEAD_COUNT = 64
KVH = 8
HEAD_SIZE = 128
R = 64
CAP = 4096
DECODED_TOKENS = 2
ROWS_ALL = 32


def draw_cache_lengths(key, part):
    key = jax.random.fold_in(key, 5)
    first_key, second_key = jax.random.split(key)
    lengths = jax.random.randint(first_key, (ROWS_ALL,), CAP // 4, CAP + 1)
    chosen = jax.random.randint(second_key, (), 0, ROWS_ALL)
    return lengths.at[chosen].set(CAP).astype(jnp.int32)


def draw_key_cache(key, part):
    key = jax.random.fold_in(key, 7)
    base_key = jax.random.fold_in(key, 0)
    keys_base = 2.5 * jax.random.truncated_normal(base_key, -6.0, 6.0, (ROWS_ALL, CAP, KVH * HEAD_SIZE), jnp.float32)
    return keys_base.astype(jnp.bfloat16)


def steps_of(rng, dims, cuts, low, high):
    loudness, own = 1.0, jax.random.fold_in(rng, 6)
    for position, shards_of in cuts:
        steps = jnp.exp(jax.random.uniform(jax.random.fold_in(own, position), (shards_of,), jnp.float32, low / len(cuts), high / len(cuts)))
        loudness = loudness * jnp.repeat(steps, dims[position] // shards_of).reshape([-1 if axis == position else 1 for axis in range(len(dims))])
    return loudness


def bell_draw(rng, extent, scale, most, cuts=(), kind=jnp.bfloat16):
    values = scale * jax.random.normal(rng, extent, jnp.float32)
    if cuts:
        values = values * steps_of(rng, extent, cuts, -0.22, 0.18)
    return jnp.clip(values, -most, most).astype(kind)


def setup_inputs(seed: int = 0) -> dict:
    splits = jax.random.split(jax.random.key(seed), 11)
    hidden_in = bell_draw(splits[0], (ROWS_ALL, DECODED_TOKENS, D), 1.0, 6.0, ((0, 16),))
    frozen_query_matrix = bell_draw(splits[1], (D, QUERY_HEAD_COUNT * HEAD_SIZE), D ** -0.5, 0.078125, ((1, 32),))
    factor_down = bell_draw(splits[2], (D, R), D ** -0.5, 0.078125, ((0, 16),))
    factor_up = bell_draw(splits[3], (R, QUERY_HEAD_COUNT * HEAD_SIZE), R ** -0.5, 0.75, ((0, 16), (1, 32)))
    query_gain = jnp.clip(1.0 + 0.18 * jax.random.normal(splits[4], (HEAD_SIZE,), jnp.float32), 0.1, 1.9)
    key_cache = draw_key_cache(jax.random.fold_in(splits[10], 71), 0)
    value_cache = bell_draw(splits[6], (ROWS_ALL, CAP, KVH * HEAD_SIZE), 1.0, 6.0, ((0, 16), (1, 4), (2, 8)))
    new_keys = bell_draw(splits[7], (ROWS_ALL, DECODED_TOKENS, KVH * HEAD_SIZE), 2.5, 15.0, ((0, 16), (2, 8)))
    new_values = bell_draw(splits[8], (ROWS_ALL, DECODED_TOKENS, KVH * HEAD_SIZE), 1.0, 6.0, ((0, 16), (2, 8)))
    cache_lengths = draw_cache_lengths(jax.random.fold_in(splits[10], 71), 0)
    return dict(hidden_in=hidden_in, frozen_query_matrix=frozen_query_matrix, factor_down=factor_down, factor_up=factor_up, query_gain=query_gain, key_cache=key_cache, value_cache=value_cache, new_keys=new_keys, new_values=new_values, cache_lengths=cache_lengths)


adapter_scale = 2.0
norm_epsilon = 1e-06
masked_score = -1e+30

def normalize_heads(query_rows, query_gain):
    spread = lax.optimization_barrier(jnp.mean(query_rows * query_rows, axis=-1, keepdims=True))
    return query_rows * lax.rsqrt(spread + norm_epsilon) * query_gain

def reference(hidden_in, frozen_query_matrix, factor_down, factor_up, query_gain, key_cache, value_cache, new_keys, new_values, cache_lengths):
    batch_row_count = hidden_in.shape[0]
    tokens_flat = hidden_in.reshape(batch_row_count * DECODED_TOKENS, D)
    frozen_portion = jnp.dot(tokens_flat, frozen_query_matrix, preferred_element_type=jnp.float32)
    low_rank = jnp.dot(tokens_flat, factor_down, preferred_element_type=jnp.float32)
    adapter_portion = jnp.dot(low_rank, factor_up.astype(jnp.float32), precision=lax.Precision.HIGHEST)
    query_rows = (frozen_portion + adapter_scale * adapter_portion).reshape(batch_row_count, DECODED_TOKENS, QUERY_HEAD_COUNT, HEAD_SIZE)
    normed = normalize_heads(query_rows, query_gain).astype(jnp.bfloat16)
    group = QUERY_HEAD_COUNT // KVH
    positions = jnp.arange(CAP + DECODED_TOKENS, dtype=jnp.int32)
    decoded = jnp.arange(DECODED_TOKENS, dtype=jnp.int32)

    def one_row(packed):
        row_query, row_keys, row_values, fresh_keys, fresh_values, length = packed
        grouped = row_query.reshape(DECODED_TOKENS, KVH, group, HEAD_SIZE).astype(jnp.float32)
        keys_all = jnp.concatenate([row_keys, fresh_keys], axis=0).reshape(CAP + DECODED_TOKENS, KVH, HEAD_SIZE).astype(jnp.float32)
        values_all = jnp.concatenate([row_values, fresh_values], axis=0).reshape(CAP + DECODED_TOKENS, KVH, HEAD_SIZE).astype(jnp.float32)
        scores = jnp.einsum('nkgd,ckd->nkgc', grouped, keys_all) * HEAD_SIZE ** (-0.5)
        in_cache = positions[None, :] < length
        fresh_ok = positions[None, :] - CAP <= decoded[:, None]
        valid = jnp.where(positions[None, :] < CAP, in_cache, fresh_ok)[:, None, None, :]
        scores = jnp.where(valid, scores, masked_score)
        highest = lax.optimization_barrier(jnp.max(scores, axis=-1, keepdims=True))
        weights = jnp.where(valid, jnp.exp(scores - highest), 0.0)
        total = lax.optimization_barrier(jnp.sum(weights, axis=-1))
        rounded = lax.optimization_barrier(weights.astype(jnp.bfloat16)).astype(jnp.float32)
        mixed = jnp.einsum('nkgc,ckd->nkgd', rounded, values_all)
        return (mixed / total[..., None]).reshape(DECODED_TOKENS, QUERY_HEAD_COUNT * HEAD_SIZE).astype(jnp.bfloat16)
    return lax.map(one_row, (normed, key_cache, value_cache, new_keys, new_values, cache_lengths))
```

```python
import jax
import jax.numpy as jnp
from jax import lax
from jax.experimental import pallas as pl
from jax.experimental.pallas import tpu as pltpu
from jax.sharding import PartitionSpec as P

adapter_scale = 2.0
norm_epsilon = 1e-06
masked_score = -1e30

NT = (((1,), (1,)), ((), ()))
NN = (((1,), (0,)), ((), ()))
f32, bf16 = jnp.float32, jnp.bfloat16


def dot(a, b, dims):
    return lax.dot_general(a, b, dims, preferred_element_type=f32)


def iota(shape, axis):
    return lax.broadcasted_iota(jnp.int32, shape, axis)


def split3(x):
    hi = x.astype(bf16)
    rest = x - hi.astype(f32)
    mid = rest.astype(bf16)
    lo = (rest - mid.astype(f32)).astype(bf16)
    return hi, mid, lo


def pack_factors(down_ref, up_ref, out_ref, padded):
    f = lax.axis_index("fsdp")
    odd = lax.rem(lax.axis_index("rep"), 2)
    padded[0:320, :] = down_ref[...]
    padded[320:384, :] = jnp.zeros((64, 64), bf16)
    pick = (iota((16, 64), 1) == iota((16, 64), 0) + 16 * f).astype(f32).astype(bf16)
    columns = dot(pick, padded[...], NT)
    spread = (iota((16, 4), 0) % 4 == iota((16, 4), 1)).astype(f32).astype(bf16)
    rows = dot(spread, up_ref[...], NN)
    rows = jnp.where(iota((16, 256), 1) // 64 == iota((16, 256), 0) // 4, rows, 0.0)
    rows = rows[:, :128] + rows[:, 128:]
    rows = rows + pltpu.roll(rows, 64, 1)
    last = jnp.where(iota((16, 128), 1) >= 64, rows, columns[:, 256:])
    whole = jnp.concatenate([columns[:, :256], last], axis=1)
    whole = jnp.where(odd == 1, pltpu.roll(whole, 64, 1), whole).astype(bf16)
    for i in range(16):
        out_ref[i] = whole


def pack_queries(hidden_ref, frozen_ref, factors_ref, out_ref, tokens, spread):
    f = lax.axis_index("fsdp")
    tokens[0:2, :] = hidden_ref[0].astype(f32)
    tokens[2:4, :] = hidden_ref[1].astype(f32)
    lane = iota((16, 384), 1)
    half = iota((16, 128), 1)
    row = iota((16, 256), 0)
    group = iota((16, 256), 1) // 64
    low = jnp.zeros((4, 16), f32)
    for rep in range(16):
        start = 640 * (rep // 2) + 256 * (rep % 2)
        part = factors_ref[rep].astype(f32)
        if rep % 2 == 0:
            columns = jnp.where(lane < 320, part, 0.0)
            rows = jnp.where(half >= 64, part[:, 256:], 0.0)
        else:
            columns = jnp.where(lane >= 64, part, 0.0)
            rows = jnp.where(half < 64, part[:, :128], 0.0)
        low += dot(tokens[:, start : start + 384].astype(bf16), columns.astype(bf16), NT)
        rows = rows + pltpu.roll(rows, 64, 1)
        rows = jnp.concatenate([rows, rows], axis=1)
        spread[16 * rep : 16 * rep + 16, :] = jnp.where(group == row // 4, rows, 0.0).astype(bf16)
    line, place = iota((64, 256), 0), iota((64, 256), 1)
    pick = ((place // 16 == line // 4) & (place % 4 == line % 4)).astype(f32).astype(bf16)
    out_ref[0:64, :] = dot(pick, spread[...], NN).astype(bf16)
    own = frozen_ref[...]
    terms = [t.astype(f32) for t in split3(own)]
    lanes = jnp.zeros((4, 256), f32)
    for i, term in enumerate(split3(low)):
        put = (iota((16, 256), 1) == iota((16, 256), 0) + 16 * f + 64 * i).astype(f32).astype(bf16)
        lanes += dot(term, put, NN)
    out_ref[64:80, :] = jnp.concatenate(terms + [lanes], axis=0).astype(bf16)


def attend(parts_ref, gain_ref, keys_ref, values_ref, new_keys_ref, new_values_ref, lengths_ref, out_ref, queries, fresh_k, fresh_v):
    f = lax.axis_index("fsdp")
    gain = gain_ref[...]
    tails = [parts_ref[i, 64:80, :].astype(f32) for i in range(4)]
    low = tails[0][12:16] + tails[1][12:16] + tails[2][12:16] + tails[3][12:16]
    low = low.astype(bf16)
    for i in range(4):
        up = parts_ref[i, 0:64, :]
        up = jnp.concatenate([up] * 4, axis=0)
        tail = tails[i]
        query = tail[0:4] + tail[4:8] + tail[8:12] + adapter_scale * dot(low, up, NN)
        for j in range(2):
            head = query[:, 128 * j : 128 * j + 128]
            mean = jnp.mean(head * head, axis=-1, keepdims=True)
            at = 8 * i + 4 * j
            queries[at : at + 4, :] = head * lax.rsqrt(mean + norm_epsilon) * gain
    normed = queries[...].astype(bf16)
    span = keys_ref.shape[1]
    fresh_k[...] = jnp.zeros_like(fresh_k)
    fresh_v[...] = jnp.zeros_like(fresh_v)
    for i in range(2):
        fresh_k[2 * i : 2 * i + 2, :] = new_keys_ref[i].astype(f32)
        fresh_v[2 * i : 2 * i + 2, :] = new_values_ref[i].astype(f32)
    scale = 128 ** (-0.5)
    first = iota((32, span), 0) % 4 < 2
    scores = jnp.where(first, dot(normed, keys_ref[0], NT), dot(normed, keys_ref[1], NT)) * scale
    limit = jnp.where(first, lengths_ref[0], lengths_ref[1])
    valid = iota((32, span), 1) + f * span < limit
    scores = jnp.where(valid, scores, masked_score)
    line, place = iota((32, 128), 0), iota((32, 128), 1)
    fresh = dot(normed, fresh_k[...].astype(bf16), NT) * scale
    fresh_valid = (place // 2 == (line % 4) // 2) & (place % 2 <= line % 2) & (f == 0)
    fresh = jnp.where(fresh_valid, fresh, masked_score)
    top = jnp.maximum(jnp.max(scores, axis=-1, keepdims=True), jnp.max(fresh, axis=-1, keepdims=True))
    weights = jnp.where(valid, jnp.exp(scores - top), 0.0)
    fresh_weights = jnp.where(fresh_valid, jnp.exp(fresh - top), 0.0)
    total = jnp.sum(weights, axis=-1, keepdims=True) + jnp.sum(fresh_weights, axis=-1, keepdims=True)
    mixed = (
        dot(jnp.where(first, weights, 0.0).astype(bf16), values_ref[0], NN)
        + dot(jnp.where(first, 0.0, weights).astype(bf16), values_ref[1], NN)
        + dot(fresh_weights.astype(bf16), fresh_v[...].astype(bf16), NN)
    )
    stats = jnp.where(iota((32, 128), 1) < 64, top, total)
    for i in range(4):
        out_ref[i, 0:8, :] = mixed[8 * i : 8 * i + 8]
        out_ref[i, 8:16, :] = stats[8 * i : 8 * i + 8]


def merge(parts_ref, out_ref):
    tops = [parts_ref[i, 8:16, 0:1] for i in range(4)]
    top = jnp.maximum(jnp.maximum(tops[0], tops[1]), jnp.maximum(tops[2], tops[3]))
    total = jnp.zeros((8, 1), f32)
    mixed = jnp.zeros((8, 128), f32)
    for i in range(4):
        scale = jnp.exp(tops[i] - top)
        total += scale * parts_ref[i, 8:16, 64:65]
        mixed += scale * parts_ref[i, 0:8, :]
    result = mixed / total
    for i in range(2):
        for j in range(2):
            out_ref[i, :, 128 * j : 128 * j + 128] = result[4 * j + 2 * i : 4 * j + 2 * i + 2].astype(bf16)


def whole(n):
    return [pl.BlockSpec(memory_space=pltpu.VMEM)] * n


def on_device(
    hidden_in,
    frozen_query_matrix,
    factor_down,
    factor_up,
    query_gain,
    key_cache,
    value_cache,
    new_keys,
    new_values,
    cache_lengths,
):
    packed = pl.pallas_call(
        pack_factors,
        out_shape=jax.ShapeDtypeStruct((16, 16, 384), bf16),
        in_specs=whole(2),
        out_specs=whole(1)[0],
        scratch_shapes=[pltpu.VMEM((384, 64), bf16)],
        name="pack_factors",
    )(factor_down, factor_up)
    factors = lax.all_to_all(packed, "rep", 0, 0)
    frozen = jnp.dot(
        hidden_in.reshape(4, 5120), frozen_query_matrix, preferred_element_type=f32
    )
    sent = pl.pallas_call(
        pack_queries,
        out_shape=jax.ShapeDtypeStruct((80, 256), bf16),
        in_specs=whole(3),
        out_specs=whole(1)[0],
        scratch_shapes=[pltpu.VMEM((4, 5120), f32), pltpu.VMEM((256, 256), bf16)],
        name="pack_queries",
    )(hidden_in, frozen, factors)
    parts = lax.all_to_all(jnp.broadcast_to(sent, (4, 80, 256)), "fsdp", 0, 0)
    partial = pl.pallas_call(
        attend,
        out_shape=jax.ShapeDtypeStruct((4, 16, 128), f32),
        in_specs=whole(6) + [pl.BlockSpec(memory_space=pltpu.SMEM)],
        out_specs=whole(1)[0],
        scratch_shapes=[pltpu.VMEM((32, 128), f32)] + [pltpu.VMEM((128, 128), f32)] * 2,
        name="attend",
    )(parts, query_gain.reshape(1, 128), key_cache, value_cache, new_keys, new_values, cache_lengths)
    partial = lax.all_to_all(partial, "fsdp", 0, 0)
    return pl.pallas_call(
        merge,
        out_shape=jax.ShapeDtypeStruct((2, 2, 256), bf16),
        in_specs=whole(1),
        out_specs=whole(1)[0],
        name="merge",
    )(partial)


def solution(mesh):
    placed = (
        P("rep", None, None),
        P(None, ("tp", "fsdp")),
        P("rep", None),
        P("rep", ("tp", "fsdp")),
        P(),
        P("rep", "fsdp", "tp"),
        P("rep", "fsdp", "tp"),
        P("rep", None, "tp"),
        P("rep", None, "tp"),
        P("rep"),
    )
    return jax.shard_map(
        on_device,
        mesh=mesh,
        in_specs=placed,
        out_specs=P("rep", None, ("tp", "fsdp")),
        check_vma=False,
    )
```

```python
import jax
import jax.numpy as jnp
from jax import lax
from jax.experimental import pallas as pl
from jax.experimental.pallas import tpu as pltpu
from jax.sharding import PartitionSpec as P

adapter_scale = 2.0
norm_epsilon = 1e-06
masked_score = -1e30

NT = (((1,), (1,)), ((), ()))
NN = (((1,), (0,)), ((), ()))
f32, bf16 = jnp.float32, jnp.bfloat16


def dot(a, b, dims):
    return lax.dot_general(a, b, dims, preferred_element_type=f32)


def iota(shape, axis):
    return lax.broadcasted_iota(jnp.int32, shape, axis)


def split3(x):
    hi = x.astype(bf16)
    rest = x - hi.astype(f32)
    mid = rest.astype(bf16)
    lo = (rest - mid.astype(f32)).astype(bf16)
    return hi, mid, lo


def pack_factors(down_ref, up_ref, out_ref):
    start = pl.multiple_of(16 * lax.axis_index("fsdp"), 16)
    odd = lax.rem(lax.axis_index("rep"), 2)
    columns = down_ref[pl.ds(start, 16), :].astype(f32)
    spread = (iota((16, 4), 0) % 4 == iota((16, 4), 1)).astype(f32).astype(bf16)
    rows = dot(spread, up_ref[...], NN)
    rows = jnp.where(iota((16, 256), 1) // 64 == iota((16, 256), 0) // 4, rows, 0.0)
    rows = rows[:, :128] + rows[:, 128:]
    rows = rows + pltpu.roll(rows, 64, 1)
    last = jnp.concatenate([columns[:, 256:], rows[:, :64]], axis=1)
    even_tiles = [columns[:, :128], columns[:, 128:256], last]
    turned = [pltpu.roll(tile, 64, 1) for tile in even_tiles]
    low = iota((16, 128), 1) < 64
    odd_tiles = [jnp.where(low, turned[i - 1], turned[i]) for i in range(3)]
    for i in range(3):
        tile = jnp.where(odd == 1, odd_tiles[i], even_tiles[i]).astype(bf16)
        for peer in range(16):
            out_ref[peer, :, 128 * i : 128 * i + 128] = tile


def pack_queries(tokens_ref, frozen_ref, factors_ref, out_ref, columns, spread):
    f = lax.axis_index("fsdp")
    low_half = iota((16, 128), 1) < 64
    here = iota((16, 256), 1) // 64 == iota((16, 256), 0) // 4
    for pair in range(8):
        even, odd = factors_ref.at[2 * pair], factors_ref.at[2 * pair + 1]
        at = 640 * pair
        columns[:, at : at + 256] = even[:, 0:256]
        columns[:, at + 384 : at + 640] = odd[:, 128:384]
        last, first = even[:, 256:384].astype(f32), odd[:, 0:128].astype(f32)
        columns[:, at + 256 : at + 384] = jnp.where(low_half, last, first).astype(bf16)
        rows = jnp.where(low_half, first, last)
        turned = pltpu.roll(rows, 64, 1)
        for i, tile in enumerate((jnp.where(low_half, turned, rows), jnp.where(low_half, rows, turned))):
            tile = jnp.where(here, jnp.concatenate([tile, tile], axis=1), 0.0)
            spread[32 * pair + 16 * i : 32 * pair + 16 * i + 16, :] = tile.astype(bf16)
    low = dot(tokens_ref[...], columns[...], NT)
    line, place = iota((64, 256), 0), iota((64, 256), 1)
    pick = ((place // 16 == line // 4) & (place % 4 == line % 4)).astype(f32).astype(bf16)
    up = dot(pick, spread[...], NN).astype(bf16)
    terms = [t.astype(f32) for t in split3(frozen_ref[...])]
    lanes = jnp.zeros((4, 256), f32)
    for i, term in enumerate(split3(low)):
        put = (iota((16, 256), 1) == iota((16, 256), 0) + 16 * f + 64 * i).astype(f32).astype(bf16)
        lanes += dot(term, put, NN)
    tail = jnp.concatenate(terms + [lanes], axis=0).astype(bf16)
    for peer in range(4):
        out_ref[peer, 0:64, :] = up
        out_ref[peer, 64:80, :] = tail


def attend(parts_ref, gain_ref, keys_ref, values_ref, new_keys_ref, new_values_ref, lengths_ref, out_ref, queries, fresh_k, fresh_v):
    f = lax.axis_index("fsdp")
    gain = gain_ref[...]
    tails = [parts_ref[i, 64:80, :].astype(f32) for i in range(4)]
    low = tails[0][12:16] + tails[1][12:16] + tails[2][12:16] + tails[3][12:16]
    low = low.astype(bf16)
    for i in range(4):
        up = parts_ref[i, 0:64, :]
        up = jnp.concatenate([up] * 4, axis=0)
        tail = tails[i]
        query = tail[0:4] + tail[4:8] + tail[8:12] + adapter_scale * dot(low, up, NN)
        for j in range(2):
            head = query[:, 128 * j : 128 * j + 128]
            mean = jnp.mean(head * head, axis=-1, keepdims=True)
            at = 8 * i + 4 * j
            queries[at : at + 4, :] = head * lax.rsqrt(mean + norm_epsilon) * gain
    normed = queries[...].astype(bf16)
    span = keys_ref.shape[1]
    fresh_k[...] = jnp.zeros_like(fresh_k)
    fresh_v[...] = jnp.zeros_like(fresh_v)
    for i in range(2):
        fresh_k[2 * i : 2 * i + 2, :] = new_keys_ref[i].astype(f32)
        fresh_v[2 * i : 2 * i + 2, :] = new_values_ref[i].astype(f32)
    scale = 128 ** (-0.5)
    first = iota((32, span), 0) % 4 < 2
    scores = jnp.where(first, dot(normed, keys_ref[0], NT), dot(normed, keys_ref[1], NT)) * scale
    limit = jnp.where(first, lengths_ref[0], lengths_ref[1])
    valid = iota((32, span), 1) + f * span < limit
    scores = jnp.where(valid, scores, masked_score)
    line, place = iota((32, 128), 0), iota((32, 128), 1)
    fresh = dot(normed, fresh_k[...].astype(bf16), NT) * scale
    fresh_valid = (place // 2 == (line % 4) // 2) & (place % 2 <= line % 2) & (f == 0)
    fresh = jnp.where(fresh_valid, fresh, masked_score)
    top = jnp.maximum(jnp.max(scores, axis=-1, keepdims=True), jnp.max(fresh, axis=-1, keepdims=True))
    weights = jnp.where(valid, jnp.exp(scores - top), 0.0)
    fresh_weights = jnp.where(fresh_valid, jnp.exp(fresh - top), 0.0)
    total = jnp.sum(weights, axis=-1, keepdims=True) + jnp.sum(fresh_weights, axis=-1, keepdims=True)
    mixed = (
        dot(jnp.where(first, weights, 0.0).astype(bf16), values_ref[0], NN)
        + dot(jnp.where(first, 0.0, weights).astype(bf16), values_ref[1], NN)
        + dot(fresh_weights.astype(bf16), fresh_v[...].astype(bf16), NN)
    )
    stats = jnp.where(iota((32, 128), 1) < 64, top, total)
    for i in range(4):
        out_ref[i, 0:8, :] = mixed[8 * i : 8 * i + 8]
        out_ref[i, 8:16, :] = stats[8 * i : 8 * i + 8]


def merge(parts_ref, out_ref):
    tops = [parts_ref[i, 8:16, 0:1] for i in range(4)]
    top = jnp.maximum(jnp.maximum(tops[0], tops[1]), jnp.maximum(tops[2], tops[3]))
    total = jnp.zeros((8, 1), f32)
    mixed = jnp.zeros((8, 128), f32)
    for i in range(4):
        scale = jnp.exp(tops[i] - top)
        total += scale * parts_ref[i, 8:16, 64:65]
        mixed += scale * parts_ref[i, 0:8, :]
    result = mixed / total
    for i in range(2):
        for j in range(2):
            out_ref[i, :, 128 * j : 128 * j + 128] = result[4 * j + 2 * i : 4 * j + 2 * i + 2].astype(bf16)


room = pltpu.CompilerParams(vmem_limit_bytes=8 * 2**20)


def whole(n):
    return [pl.BlockSpec(memory_space=pltpu.VMEM)] * n


def on_device(
    hidden_in,
    frozen_query_matrix,
    factor_down,
    factor_up,
    query_gain,
    key_cache,
    value_cache,
    new_keys,
    new_values,
    cache_lengths,
):
    packed = pl.pallas_call(
        pack_factors,
        out_shape=jax.ShapeDtypeStruct((16, 16, 384), bf16),
        in_specs=whole(2),
        out_specs=whole(1)[0],
        compiler_params=room,
        name="pack_factors",
    )(factor_down.T, factor_up)
    factors = lax.all_to_all(packed, "rep", 0, 0)
    tokens = hidden_in.reshape(4, 5120)
    frozen = jnp.dot(tokens, frozen_query_matrix, preferred_element_type=f32)
    sent = pl.pallas_call(
        pack_queries,
        out_shape=jax.ShapeDtypeStruct((4, 80, 256), bf16),
        in_specs=whole(3),
        out_specs=whole(1)[0],
        scratch_shapes=[pltpu.VMEM((16, 5120), bf16), pltpu.VMEM((256, 256), bf16)],
        compiler_params=room,
        name="pack_queries",
    )(tokens, frozen, factors)
    parts = lax.all_to_all(sent, "fsdp", 0, 0)
    partial = pl.pallas_call(
        attend,
        out_shape=jax.ShapeDtypeStruct((4, 16, 128), f32),
        in_specs=whole(6) + [pl.BlockSpec(memory_space=pltpu.SMEM)],
        out_specs=whole(1)[0],
        scratch_shapes=[pltpu.VMEM((32, 128), f32)] + [pltpu.VMEM((128, 128), f32)] * 2,
        compiler_params=room,
        name="attend",
    )(parts, query_gain.reshape(1, 128), key_cache, value_cache, new_keys, new_values, cache_lengths)
    partial = lax.all_to_all(partial, "fsdp", 0, 0)
    return pl.pallas_call(
        merge,
        out_shape=jax.ShapeDtypeStruct((2, 2, 256), bf16),
        in_specs=whole(1),
        out_specs=whole(1)[0],
        compiler_params=room,
        name="merge",
    )(partial)


def solution(mesh):
    placed = (
        P("rep", None, None),
        P(None, ("tp", "fsdp")),
        P("rep", None),
        P("rep", ("tp", "fsdp")),
        P(),
        P("rep", "fsdp", "tp"),
        P("rep", "fsdp", "tp"),
        P("rep", None, "tp"),
        P("rep", None, "tp"),
        P("rep"),
    )
    return jax.shard_map(
        on_device,
        mesh=mesh,
        in_specs=placed,
        out_specs=P("rep", None, ("tp", "fsdp")),
        check_vma=False,
    )
```

```python
import jax
import jax.numpy as jnp
from jax import lax
from jax.experimental import pallas as pl
from jax.experimental.pallas import tpu as pltpu
from jax.sharding import PartitionSpec as P

adapter_scale = 2.0
norm_epsilon = 1e-06
masked_score = -1e30

NT = (((1,), (1,)), ((), ()))
NN = (((1,), (0,)), ((), ()))
f32, bf16 = jnp.float32, jnp.bfloat16


def dot(a, b, dims):
    return lax.dot_general(a, b, dims, preferred_element_type=f32)


def iota(shape, axis):
    return lax.broadcasted_iota(jnp.int32, shape, axis)


def split3(x):
    hi = x.astype(bf16)
    rest = x - hi.astype(f32)
    mid = rest.astype(bf16)
    lo = (rest - mid.astype(f32)).astype(bf16)
    return hi, mid, lo


def pack_factors(down_hbm, up_hbm, out_ref, down_ref, up_ref, rows_ref, sems):
    start = pl.multiple_of(16 * lax.axis_index("fsdp"), 16)
    odd = lax.rem(lax.axis_index("rep"), 2)
    down_copy = pltpu.make_async_copy(down_hbm.at[pl.ds(start, 16), :], down_ref, sems.at[0])
    up_copy = pltpu.make_async_copy(up_hbm, up_ref, sems.at[1])
    down_copy.start()
    up_copy.start()
    up_copy.wait()
    up = up_ref[...].astype(f32)
    for i in range(2):
        half = up[:, 128 * i : 128 * i + 128]
        turned = pltpu.roll(half, 64, 1)
        rows_ref[8 * i : 8 * i + 4, :] = jnp.where(odd == 1, half, turned)
        rows_ref[8 * i + 4 : 8 * i + 8, :] = jnp.where(odd == 1, turned, half)
    down_copy.wait()
    columns = down_ref[...].astype(f32)
    last = jnp.concatenate([columns[:, 256:], jnp.zeros((16, 64), f32)], axis=1)
    low = iota((16, 128), 1) < 64
    even_tiles = [columns[:, :128], columns[:, 128:256], jnp.where(low, last, rows_ref[...])]
    turned = [pltpu.roll(tile, 64, 1) for tile in (columns[:, :128], columns[:, 128:256], last)]
    odd_tiles = [jnp.where(low, rows_ref[...], turned[0])]
    odd_tiles += [jnp.where(low, turned[i - 1], turned[i]) for i in (1, 2)]
    for i in range(3):
        tile = jnp.where(odd == 1, odd_tiles[i], even_tiles[i]).astype(bf16)
        for peer in range(16):
            out_ref[peer, :, 128 * i : 128 * i + 128] = tile


def project(hidden_ref, frozen_ref, keys_hbm, values_hbm, tokens_ref, terms_ref, keys_ref, values_ref, sems):
    keys_copy = pltpu.make_async_copy(keys_hbm, keys_ref, sems.at[0])
    values_copy = pltpu.make_async_copy(values_hbm, values_ref, sems.at[1])
    keys_copy.start()
    values_copy.start()
    tokens = jnp.concatenate([hidden_ref[0].astype(f32), hidden_ref[1].astype(f32)], axis=0)
    tokens = tokens.astype(bf16)
    tokens_ref[...] = tokens
    terms = [t.astype(f32) for t in split3(dot(tokens, frozen_ref[...], NN))]
    terms_ref[...] = jnp.concatenate(terms + [jnp.zeros((4, 256), f32)], axis=0)
    keys_copy.wait()
    values_copy.wait()


def pack_queries(tokens_ref, terms_ref, factors_ref, out_ref, columns, spread):
    f = lax.axis_index("fsdp")
    low_half = iota((16, 128), 1) < 64
    here = iota((16, 256), 1) // 64 == iota((16, 256), 0) // 4
    for pair in range(8):
        even, odd = factors_ref.at[2 * pair], factors_ref.at[2 * pair + 1]
        at = 640 * pair
        columns[:, at : at + 256] = even[:, 0:256]
        columns[:, at + 384 : at + 640] = odd[:, 128:384]
        last, first = even[:, 256:384].astype(f32), odd[:, 0:128].astype(f32)
        columns[:, at + 256 : at + 384] = jnp.where(low_half, last, first).astype(bf16)
        rows = jnp.where(low_half, first, last)
        turned = pltpu.roll(rows, 64, 1)
        for i, tile in enumerate((jnp.where(low_half, turned, rows), jnp.where(low_half, rows, turned))):
            tile = jnp.where(here, jnp.concatenate([tile, tile], axis=1), 0.0)
            spread[32 * pair + 16 * i : 32 * pair + 16 * i + 16, :] = tile.astype(bf16)
    low = dot(tokens_ref[...], columns[...], NT)
    line, place = iota((64, 256), 0), iota((64, 256), 1)
    pick = ((place // 16 == line // 4) & (place % 4 == line % 4)).astype(f32).astype(bf16)
    up = dot(pick, spread[...], NN).astype(bf16)
    lanes = jnp.zeros((4, 256), f32)
    for i, term in enumerate(split3(low)):
        put = (iota((16, 256), 1) == iota((16, 256), 0) + 16 * f + 64 * i).astype(f32).astype(bf16)
        lanes += dot(term, put, NN)
    tail = jnp.concatenate([terms_ref[0:12, :], lanes], axis=0).astype(bf16)
    for peer in range(4):
        out_ref[peer, 0:64, :] = up
        out_ref[peer, 64:80, :] = tail


def attend(parts_ref, gain_ref, keys_ref, values_ref, new_keys_ref, new_values_ref, lengths_ref, out_ref, queries, fresh_k, fresh_v):
    f = lax.axis_index("fsdp")
    gain = gain_ref[...]
    tails = [parts_ref[i, 64:80, :].astype(f32) for i in range(4)]
    low = tails[0][12:16] + tails[1][12:16] + tails[2][12:16] + tails[3][12:16]
    low = low.astype(bf16)
    for i in range(4):
        up = parts_ref[i, 0:64, :]
        up = jnp.concatenate([up] * 4, axis=0)
        tail = tails[i]
        query = tail[0:4] + tail[4:8] + tail[8:12] + adapter_scale * dot(low, up, NN)
        for j in range(2):
            head = query[:, 128 * j : 128 * j + 128]
            mean = jnp.mean(head * head, axis=-1, keepdims=True)
            at = 8 * i + 4 * j
            queries[at : at + 4, :] = head * lax.rsqrt(mean + norm_epsilon) * gain
    normed = queries[...].astype(bf16)
    span = keys_ref.shape[1]
    fresh_k[...] = jnp.zeros_like(fresh_k)
    fresh_v[...] = jnp.zeros_like(fresh_v)
    for i in range(2):
        fresh_k[2 * i : 2 * i + 2, :] = new_keys_ref[i].astype(f32)
        fresh_v[2 * i : 2 * i + 2, :] = new_values_ref[i].astype(f32)
    scale = 128 ** (-0.5)
    first = iota((32, span), 0) % 4 < 2
    scores = jnp.where(first, dot(normed, keys_ref[0], NT), dot(normed, keys_ref[1], NT)) * scale
    limit = jnp.where(first, lengths_ref[0], lengths_ref[1])
    valid = iota((32, span), 1) + f * span < limit
    scores = jnp.where(valid, scores, masked_score)
    line, place = iota((32, 128), 0), iota((32, 128), 1)
    fresh = dot(normed, fresh_k[...].astype(bf16), NT) * scale
    fresh_valid = (place // 2 == (line % 4) // 2) & (place % 2 <= line % 2) & (f == 0)
    fresh = jnp.where(fresh_valid, fresh, masked_score)
    top = jnp.maximum(jnp.max(scores, axis=-1, keepdims=True), jnp.max(fresh, axis=-1, keepdims=True))
    weights = jnp.where(valid, jnp.exp(scores - top), 0.0)
    fresh_weights = jnp.where(fresh_valid, jnp.exp(fresh - top), 0.0)
    total = jnp.sum(weights, axis=-1, keepdims=True) + jnp.sum(fresh_weights, axis=-1, keepdims=True)
    mixed = (
        dot(jnp.where(first, weights, 0.0).astype(bf16), values_ref[0], NN)
        + dot(jnp.where(first, 0.0, weights).astype(bf16), values_ref[1], NN)
        + dot(fresh_weights.astype(bf16), fresh_v[...].astype(bf16), NN)
    )
    stats = jnp.where(iota((32, 128), 1) < 64, top, total)
    for i in range(4):
        out_ref[i, 0:8, :] = mixed[8 * i : 8 * i + 8]
        out_ref[i, 8:16, :] = stats[8 * i : 8 * i + 8]


def merge(parts_ref, out_ref):
    tops = [parts_ref[i, 8:16, 0:1] for i in range(4)]
    top = jnp.maximum(jnp.maximum(tops[0], tops[1]), jnp.maximum(tops[2], tops[3]))
    total = jnp.zeros((8, 1), f32)
    mixed = jnp.zeros((8, 128), f32)
    for i in range(4):
        scale = jnp.exp(tops[i] - top)
        total += scale * parts_ref[i, 8:16, 64:65]
        mixed += scale * parts_ref[i, 0:8, :]
    result = mixed / total
    for i in range(2):
        for j in range(2):
            out_ref[i, :, 128 * j : 128 * j + 128] = result[4 * j + 2 * i : 4 * j + 2 * i + 2].astype(bf16)


room = pltpu.CompilerParams(vmem_limit_bytes=8 * 2**20)


def whole(n):
    return [pl.BlockSpec(memory_space=pltpu.VMEM)] * n


def on_device(
    hidden_in,
    frozen_query_matrix,
    factor_down,
    factor_up,
    query_gain,
    key_cache,
    value_cache,
    new_keys,
    new_values,
    cache_lengths,
):
    packed = pl.pallas_call(
        pack_factors,
        out_shape=jax.ShapeDtypeStruct((16, 16, 384), bf16),
        in_specs=[pl.BlockSpec(memory_space=pltpu.HBM)] * 2,
        out_specs=whole(1)[0],
        scratch_shapes=[
            pltpu.VMEM((16, 320), bf16),
            pltpu.VMEM((4, 256), bf16),
            pltpu.VMEM((16, 128), f32),
            pltpu.SemaphoreType.DMA((2,)),
        ],
        name="pack_factors",
    )(factor_down.T, factor_up)
    factors = lax.all_to_all(packed, "rep", 0, 0)
    tokens, terms, keys, values = pl.pallas_call(
        project,
        out_shape=(
            jax.ShapeDtypeStruct((4, 5120), bf16),
            jax.ShapeDtypeStruct((16, 256), f32),
            jax.ShapeDtypeStruct(key_cache.shape, bf16),
            jax.ShapeDtypeStruct(value_cache.shape, bf16),
        ),
        in_specs=whole(2) + [pl.BlockSpec(memory_space=pltpu.HBM)] * 2,
        out_specs=tuple(whole(4)),
        scratch_shapes=[pltpu.SemaphoreType.DMA((2,))],
        compiler_params=room,
        cost_estimate=pl.CostEstimate(flops=2 * 4 * 5120 * 256, bytes_accessed=8 * 2**20, transcendentals=0),
        name="project",
    )(hidden_in, frozen_query_matrix, key_cache, value_cache)
    sent = pl.pallas_call(
        pack_queries,
        out_shape=jax.ShapeDtypeStruct((4, 80, 256), bf16),
        in_specs=whole(3),
        out_specs=whole(1)[0],
        scratch_shapes=[pltpu.VMEM((16, 5120), bf16), pltpu.VMEM((256, 256), bf16)],
        compiler_params=room,
        name="pack_queries",
    )(tokens, terms, factors)
    parts = lax.all_to_all(sent, "fsdp", 0, 0)
    partial = pl.pallas_call(
        attend,
        out_shape=jax.ShapeDtypeStruct((4, 16, 128), f32),
        in_specs=whole(6) + [pl.BlockSpec(memory_space=pltpu.SMEM)],
        out_specs=whole(1)[0],
        scratch_shapes=[pltpu.VMEM((32, 128), f32)] + [pltpu.VMEM((128, 128), f32)] * 2,
        compiler_params=room,
        name="attend",
    )(parts, query_gain.reshape(1, 128), keys, values, new_keys, new_values, cache_lengths)
    partial = lax.all_to_all(partial, "fsdp", 0, 0)
    return pl.pallas_call(
        merge,
        out_shape=jax.ShapeDtypeStruct((2, 2, 256), bf16),
        in_specs=whole(1),
        out_specs=whole(1)[0],
        compiler_params=room,
        name="merge",
    )(partial)


def solution(mesh):
    placed = (
        P("rep", None, None),
        P(None, ("tp", "fsdp")),
        P("rep", None),
        P("rep", ("tp", "fsdp")),
        P(),
        P("rep", "fsdp", "tp"),
        P("rep", "fsdp", "tp"),
        P("rep", None, "tp"),
        P("rep", None, "tp"),
        P("rep"),
    )
    return jax.shard_map(
        on_device,
        mesh=mesh,
        in_specs=placed,
        out_specs=P("rep", None, ("tp", "fsdp")),
        check_vma=False,
    )
```

```python
import jax
import jax.numpy as jnp
from jax import lax
from jax.experimental import pallas as pl
from jax.experimental.pallas import tpu as pltpu
from jax.sharding import PartitionSpec as P

adapter_scale = 2.0
norm_epsilon = 1e-06
masked_score = -1e30

NT = (((1,), (1,)), ((), ()))
NN = (((1,), (0,)), ((), ()))
f32, bf16 = jnp.float32, jnp.bfloat16


def dot(a, b, dims):
    return lax.dot_general(a, b, dims, preferred_element_type=f32)


def iota(shape, axis):
    return lax.broadcasted_iota(jnp.int32, shape, axis)


def split3(x):
    hi = x.astype(bf16)
    rest = x - hi.astype(f32)
    mid = rest.astype(bf16)
    lo = (rest - mid.astype(f32)).astype(bf16)
    return hi, mid, lo


def pack_factors(down_hbm, up_hbm, out_ref, down_ref, up_ref, rows_ref, sems):
    start = pl.multiple_of(16 * lax.axis_index("fsdp"), 16)
    down_copy = pltpu.make_async_copy(down_hbm.at[pl.ds(start, 16), :], down_ref, sems.at[0])
    up_copy = pltpu.make_async_copy(up_hbm, up_ref, sems.at[1])
    down_copy.start()
    up_copy.start()
    up_copy.wait()
    up = up_ref[...].astype(f32)
    for i in range(2):
        half = up[:, 128 * i : 128 * i + 128]
        rows_ref[8 * i : 8 * i + 4, :] = pltpu.roll(half, 64, 1)
        rows_ref[8 * i + 4 : 8 * i + 8, :] = half
    down_copy.wait()
    columns = down_ref[...].astype(f32)
    last = jnp.concatenate([columns[:, 256:], jnp.zeros((16, 64), f32)], axis=1)
    last = jnp.where(iota((16, 128), 1) < 64, last, rows_ref[...])
    whole = jnp.concatenate([columns[:, :256], last], axis=1).astype(bf16)
    for peer in range(8):
        out_ref[peer] = whole


def project(hidden_hbm, frozen_hbm, keys_hbm, values_hbm, terms_ref, keys_ref, values_ref, hidden_ref, frozen_ref, sems):
    copies = [
        pltpu.make_async_copy(source, target, sems.at[i])
        for i, (source, target) in enumerate(
            (
                (hidden_hbm, hidden_ref),
                (frozen_hbm, frozen_ref),
                (keys_hbm, keys_ref),
                (values_hbm, values_ref),
            )
        )
    ]
    for copy in copies:
        copy.start()
    copies[0].wait()
    tokens = jnp.concatenate([hidden_ref[0].astype(f32), hidden_ref[1].astype(f32)], axis=0)
    copies[1].wait()
    terms = [t.astype(f32) for t in split3(dot(tokens.astype(bf16), frozen_ref[...], NN))]
    terms_ref[...] = jnp.concatenate(terms + [jnp.zeros((4, 256), f32)], axis=0)
    copies[2].wait()
    copies[3].wait()


def align(hidden_ref, other_ref, out_ref, tokens):
    upper = lax.axis_index("ylo") == 1
    for i in range(2):
        tokens[2 * i : 2 * i + 2, :] = hidden_ref[i].astype(f32)
        tokens[4 + 2 * i : 6 + 2 * i, :] = other_ref[i].astype(f32)
    low = iota((8, 128), 1) < 64
    for z in range(8):
        tiles = [tokens[:, 640 * z + 128 * i : 640 * z + 128 * i + 128] for i in range(5)]
        turned = [pltpu.roll(tile, 64, 1) for tile in tiles[2:]] + [jnp.zeros((8, 128), f32)]
        for i in range(3):
            shifted = jnp.where(low, turned[i], turned[i + 1])
            plain = tiles[i] if i < 2 else jnp.where(low, tiles[2], 0.0)
            at = 384 * z + 128 * i
            out_ref[:, at : at + 128] = jnp.where(upper, shifted, plain).astype(bf16)


def pack_queries(tokens_ref, terms_ref, factors_ref, out_ref, columns, spread):
    f, ylo = lax.axis_index("fsdp"), lax.axis_index("ylo")
    low_half = iota((16, 128), 1) < 64
    here = iota((16, 256), 1) // 64 == iota((16, 256), 0) // 4
    for z in range(8):
        columns[:, 384 * z : 384 * z + 384] = factors_ref[z]
        last = factors_ref[z, :, 256:384].astype(f32)
        rows = jnp.where(low_half, pltpu.roll(last, 64, 1), last)
        rows = jnp.where(here, jnp.concatenate([rows, rows], axis=1), 0.0)
        spread[16 * z : 16 * z + 16, :] = rows.astype(bf16)
    low = dot(tokens_ref[...], columns[...], NT)
    line, place = iota((32, 128), 0), iota((32, 128), 1)
    pick = ((place // 16 == line // 4) & (place % 4 == line % 4)).astype(f32).astype(bf16)
    up = dot(pick, spread[...], NN).astype(bf16)
    rank = iota((16, 256), 0) + 16 * f
    rank = 32 * (rank // 4 % 2) + 4 * (rank // 8) + rank % 4
    lanes = jnp.zeros((8, 256), f32)
    for i, term in enumerate(split3(low)):
        put = (iota((16, 256), 1) == rank + 64 * i).astype(f32).astype(bf16)
        lanes += dot(term, put, NN)
    for y in range(2):
        part = jnp.where(ylo == y, lanes[0:4], lanes[4:8])
        tail = jnp.concatenate([terms_ref[0:12, :], part], axis=0).astype(bf16)
        for peer in range(4):
            out_ref[2 * peer + y, 0:32, :] = up
            out_ref[2 * peer + y, 32:48, :] = tail


def attend(parts_ref, gain_ref, keys_ref, values_ref, new_keys_ref, new_values_ref, lengths_ref, out_ref, queries, fresh_k, fresh_v):
    f = lax.axis_index("fsdp")
    upper = lax.axis_index("ylo") == 1
    gain = gain_ref[...]
    tails = [parts_ref[i, 32:48, :].astype(f32) for i in range(8)]
    low = [tails[y][12:16] + tails[2 + y][12:16] + tails[4 + y][12:16] + tails[6 + y][12:16] for y in range(2)]
    low = jnp.concatenate(low, axis=0).astype(bf16)
    for i in range(4):
        up = jnp.concatenate([parts_ref[2 * i, 0:32, :], parts_ref[2 * i + 1, 0:32, :]] * 4, axis=0)
        tail = jnp.where(upper, tails[2 * i + 1], tails[2 * i])
        adapter = dot(low, up, NN)
        adapter = adapter[0:4] + adapter[4:8]
        query = tail[0:4] + tail[4:8] + tail[8:12] + adapter_scale * adapter
        for j in range(2):
            head = query[:, 128 * j : 128 * j + 128]
            mean = jnp.mean(head * head, axis=-1, keepdims=True)
            at = 8 * i + 4 * j
            queries[at : at + 4, :] = head * lax.rsqrt(mean + norm_epsilon) * gain
    normed = queries[...].astype(bf16)
    span = keys_ref.shape[1]
    fresh_k[...] = jnp.zeros_like(fresh_k)
    fresh_v[...] = jnp.zeros_like(fresh_v)
    for i in range(2):
        fresh_k[2 * i : 2 * i + 2, :] = new_keys_ref[i].astype(f32)
        fresh_v[2 * i : 2 * i + 2, :] = new_values_ref[i].astype(f32)
    scale = 128 ** (-0.5)
    first = iota((32, span), 0) % 4 < 2
    scores = jnp.where(first, dot(normed, keys_ref[0], NT), dot(normed, keys_ref[1], NT)) * scale
    limit = jnp.where(first, lengths_ref[0], lengths_ref[1])
    valid = iota((32, span), 1) + f * span < limit
    scores = jnp.where(valid, scores, masked_score)
    line, place = iota((32, 128), 0), iota((32, 128), 1)
    fresh = dot(normed, fresh_k[...].astype(bf16), NT) * scale
    fresh_valid = (place // 2 == (line % 4) // 2) & (place % 2 <= line % 2) & (f == 0)
    fresh = jnp.where(fresh_valid, fresh, masked_score)
    top = jnp.maximum(jnp.max(scores, axis=-1, keepdims=True), jnp.max(fresh, axis=-1, keepdims=True))
    weights = jnp.where(valid, jnp.exp(scores - top), 0.0)
    fresh_weights = jnp.where(fresh_valid, jnp.exp(fresh - top), 0.0)
    total = jnp.sum(weights, axis=-1, keepdims=True) + jnp.sum(fresh_weights, axis=-1, keepdims=True)
    mixed = (
        dot(jnp.where(first, weights, 0.0).astype(bf16), values_ref[0], NN)
        + dot(jnp.where(first, 0.0, weights).astype(bf16), values_ref[1], NN)
        + dot(fresh_weights.astype(bf16), fresh_v[...].astype(bf16), NN)
    )
    stats = jnp.where(iota((32, 128), 1) < 64, top, total)
    for i in range(4):
        out_ref[i, 0:8, :] = mixed[8 * i : 8 * i + 8]
        out_ref[i, 8:16, :] = stats[8 * i : 8 * i + 8]


def merge(parts_ref, out_ref):
    tops = [parts_ref[i, 8:16, 0:1] for i in range(4)]
    top = jnp.maximum(jnp.maximum(tops[0], tops[1]), jnp.maximum(tops[2], tops[3]))
    total = jnp.zeros((8, 1), f32)
    mixed = jnp.zeros((8, 128), f32)
    for i in range(4):
        scale = jnp.exp(tops[i] - top)
        total += scale * parts_ref[i, 8:16, 64:65]
        mixed += scale * parts_ref[i, 0:8, :]
    result = mixed / total
    for i in range(2):
        for j in range(2):
            out_ref[i, :, 128 * j : 128 * j + 128] = result[4 * j + 2 * i : 4 * j + 2 * i + 2].astype(bf16)


room = pltpu.CompilerParams(vmem_limit_bytes=8 * 2**20)


def whole(n):
    return [pl.BlockSpec(memory_space=pltpu.VMEM)] * n


def hbm(n):
    return [pl.BlockSpec(memory_space=pltpu.HBM)] * n


def far(x):
    return pltpu.with_memory_space_constraint(x, pltpu.HBM)


def on_device(
    hidden_in,
    frozen_query_matrix,
    factor_down,
    factor_up,
    query_gain,
    key_cache,
    value_cache,
    new_keys,
    new_values,
    cache_lengths,
):
    packed = pl.pallas_call(
        pack_factors,
        out_shape=jax.ShapeDtypeStruct((8, 16, 384), bf16),
        in_specs=hbm(2),
        out_specs=whole(1)[0],
        scratch_shapes=[
            pltpu.VMEM((16, 320), bf16),
            pltpu.VMEM((4, 256), bf16),
            pltpu.VMEM((16, 128), f32),
            pltpu.SemaphoreType.DMA((2,)),
        ],
        compiler_params=room,
        name="pack_factors",
    )(far(factor_down.T), far(factor_up))
    factors = lax.all_to_all(packed, "z", 0, 0)
    other = lax.ppermute(hidden_in, "ylo", ((0, 1), (1, 0)))
    terms, keys, values = pl.pallas_call(
        project,
        out_shape=(
            jax.ShapeDtypeStruct((16, 256), f32),
            pltpu.VMEM(key_cache.shape, bf16),
            pltpu.VMEM(value_cache.shape, bf16),
        ),
        in_specs=hbm(4),
        out_specs=tuple(whole(3)),
        scratch_shapes=[
            pltpu.VMEM((2, 2, 5120), bf16),
            pltpu.VMEM((5120, 256), bf16),
            pltpu.SemaphoreType.DMA((4,)),
        ],
        compiler_params=room,
        cost_estimate=pl.CostEstimate(flops=2 * 4 * 5120 * 256, bytes_accessed=8 * 2**20, transcendentals=0),
        name="project",
    )(far(hidden_in), far(frozen_query_matrix), far(key_cache), far(value_cache))
    aligned = pl.pallas_call(
        align,
        out_shape=jax.ShapeDtypeStruct((8, 8 * 384), bf16),
        in_specs=whole(2),
        out_specs=whole(1)[0],
        scratch_shapes=[pltpu.VMEM((8, 5120), f32)],
        compiler_params=room,
        name="align",
    )(hidden_in, other)
    sent = pl.pallas_call(
        pack_queries,
        out_shape=jax.ShapeDtypeStruct((8, 48, 256), bf16),
        in_specs=whole(3),
        out_specs=whole(1)[0],
        scratch_shapes=[pltpu.VMEM((16, 8 * 384), bf16), pltpu.VMEM((128, 256), bf16)],
        compiler_params=room,
        name="pack_queries",
    )(aligned, terms, factors)
    parts = lax.all_to_all(sent, ("fsdp", "ylo"), 0, 0)
    partial = pl.pallas_call(
        attend,
        out_shape=jax.ShapeDtypeStruct((4, 16, 128), f32),
        in_specs=whole(6) + [pl.BlockSpec(memory_space=pltpu.SMEM)],
        out_specs=whole(1)[0],
        scratch_shapes=[pltpu.VMEM((32, 128), f32)] + [pltpu.VMEM((128, 128), f32)] * 2,
        compiler_params=room,
        name="attend",
    )(parts, query_gain.reshape(1, 128), keys, values, new_keys, new_values, cache_lengths)
    partial = lax.all_to_all(partial, "fsdp", 0, 0)
    return pl.pallas_call(
        merge,
        out_shape=jax.ShapeDtypeStruct((2, 2, 256), bf16),
        in_specs=whole(1),
        out_specs=whole(1)[0],
        compiler_params=room,
        name="merge",
    )(partial)


def solution(mesh):
    rep = ("z", "ylo")
    lines = mesh.devices.reshape(mesh.devices.shape[0] // 2, 2, *mesh.devices.shape[1:])
    lines = jax.sharding.Mesh(lines, rep + mesh.axis_names[1:])
    placed = (
        P(rep, None, None),
        P(None, ("tp", "fsdp")),
        P(rep, None),
        P(rep, ("tp", "fsdp")),
        P(),
        P(rep, "fsdp", "tp"),
        P(rep, "fsdp", "tp"),
        P(rep, None, "tp"),
        P(rep, None, "tp"),
        P(rep),
    )
    return jax.shard_map(
        on_device,
        mesh=lines,
        in_specs=placed,
        out_specs=P(rep, None, ("tp", "fsdp")),
        check_vma=False,
    )
```

```python
import jax
import jax.numpy as jnp
from jax import lax
from jax.experimental import pallas as pl
from jax.experimental.pallas import tpu as pltpu
from jax.sharding import PartitionSpec as P

adapter_scale = 2.0
norm_epsilon = 1e-06
masked_score = -1e30

z_order = (6, 7, 0, 1, 2, 3, 4, 5)
y_order = (5, 6, 7, 0, 1, 2, 3, 4)
fsdp_order = (2, 3, 0, 1)

NT = (((1,), (1,)), ((), ()))
NN = (((1,), (0,)), ((), ()))
f32, bf16 = jnp.float32, jnp.bfloat16


def dot(a, b, dims):
    return lax.dot_general(a, b, dims, preferred_element_type=f32)


def iota(shape, axis):
    return lax.broadcasted_iota(jnp.int32, shape, axis)


def split3(x):
    hi = x.astype(bf16)
    rest = x - hi.astype(f32)
    mid = rest.astype(bf16)
    lo = (rest - mid.astype(f32)).astype(bf16)
    return hi, mid, lo


def pack_factors(down_hbm, up_hbm, out_ref, down_ref, up_ref, rows_ref, sems):
    start = pl.multiple_of(16 * lax.axis_index("fsdp"), 16)
    down_copy = pltpu.make_async_copy(down_hbm.at[pl.ds(start, 16), :], down_ref, sems.at[0])
    up_copy = pltpu.make_async_copy(up_hbm, up_ref, sems.at[1])
    down_copy.start()
    up_copy.start()
    up_copy.wait()
    up = up_ref[...].astype(f32)
    for i in range(2):
        half = up[:, 128 * i : 128 * i + 128]
        rows_ref[8 * i : 8 * i + 4, :] = pltpu.roll(half, 64, 1)
        rows_ref[8 * i + 4 : 8 * i + 8, :] = half
    down_copy.wait()
    columns = down_ref[...].astype(f32)
    last = jnp.concatenate([columns[:, 256:], jnp.zeros((16, 64), f32)], axis=1)
    last = jnp.where(iota((16, 128), 1) < 64, last, rows_ref[...])
    whole = jnp.concatenate([columns[:, :256], last], axis=1).astype(bf16)
    for peer in range(8):
        out_ref[peer] = whole


def project(hidden_hbm, frozen_hbm, keys_hbm, values_hbm, terms_ref, keys_ref, values_ref, hidden_ref, frozen_ref, sems):
    copies = [
        pltpu.make_async_copy(source, target, sems.at[i])
        for i, (source, target) in enumerate(
            (
                (hidden_hbm, hidden_ref),
                (frozen_hbm, frozen_ref),
                (keys_hbm, keys_ref),
                (values_hbm, values_ref),
            )
        )
    ]
    for copy in copies:
        copy.start()
    copies[0].wait()
    tokens = jnp.concatenate([hidden_ref[0].astype(f32), hidden_ref[1].astype(f32)], axis=0)
    copies[1].wait()
    terms = [t.astype(f32) for t in split3(dot(tokens.astype(bf16), frozen_ref[...], NN))]
    terms_ref[...] = jnp.concatenate(terms + [jnp.zeros((4, 256), f32)], axis=0)
    copies[2].wait()
    copies[3].wait()


def align(hidden_ref, other_ref, out_ref, tokens):
    upper = lax.axis_index("ylo") == 1
    for i in range(2):
        tokens[2 * i : 2 * i + 2, :] = hidden_ref[i].astype(f32)
        tokens[4 + 2 * i : 6 + 2 * i, :] = other_ref[i].astype(f32)
    low = iota((8, 128), 1) < 64
    for peer, z in enumerate(z_order):
        tiles = [tokens[:, 640 * z + 128 * i : 640 * z + 128 * i + 128] for i in range(5)]
        turned = [pltpu.roll(tile, 64, 1) for tile in tiles[2:]] + [jnp.zeros((8, 128), f32)]
        for i in range(3):
            shifted = jnp.where(low, turned[i], turned[i + 1])
            plain = tiles[i] if i < 2 else jnp.where(low, tiles[2], 0.0)
            at = 384 * peer + 128 * i
            out_ref[:, at : at + 128] = jnp.where(upper, shifted, plain).astype(bf16)


def pack_queries(tokens_ref, terms_ref, factors_ref, out_ref, columns, spread):
    f, ylo = lax.axis_index("fsdp"), lax.axis_index("ylo")
    low_half = iota((16, 128), 1) < 64
    here = iota((16, 256), 1) // 64 == iota((16, 256), 0) // 4
    for z in range(8):
        columns[:, 384 * z : 384 * z + 384] = factors_ref[z]
        last = factors_ref[z, :, 256:384].astype(f32)
        rows = jnp.where(low_half, pltpu.roll(last, 64, 1), last)
        rows = jnp.where(here, jnp.concatenate([rows, rows], axis=1), 0.0)
        spread[16 * z : 16 * z + 16, :] = rows.astype(bf16)
    low = dot(tokens_ref[...], columns[...], NT)
    line, place = iota((32, 128), 0), iota((32, 128), 1)
    pick = jnp.zeros((32, 128), jnp.bool_)
    for peer, z in enumerate(z_order):
        pick |= (place // 16 == peer) & (line // 4 == z) & (place % 4 == line % 4)
    pick = pick.astype(f32).astype(bf16)
    up = dot(pick, spread[...], NN).astype(bf16)
    rank = iota((16, 256), 0) + 16 * f
    rank = 32 * (rank // 4 % 2) + 4 * (rank // 8) + rank % 4
    lanes = jnp.zeros((8, 256), f32)
    for i, term in enumerate(split3(low)):
        put = (iota((16, 256), 1) == rank + 64 * i).astype(f32).astype(bf16)
        lanes += dot(term, put, NN)
    tails = []
    for y in range(2):
        part = jnp.where(ylo == y, lanes[0:4], lanes[4:8])
        tails.append(jnp.concatenate([terms_ref[0:12, :], part], axis=0).astype(bf16))
    for peer, y in enumerate(y_order):
        out_ref[peer, 0:32, :] = up
        out_ref[peer, 32:48, :] = tails[y % 2]


def attend(parts_ref, gain_ref, keys_ref, values_ref, new_keys_ref, new_values_ref, lengths_ref, out_ref, queries, fresh_k, fresh_v):
    f = lax.axis_index("fsdp")
    upper = lax.axis_index("ylo") == 1
    gain = gain_ref[...]
    peers = [y_order.index(y) for y in range(8)]
    tails = [parts_ref[i, 32:48, :].astype(f32) for i in peers]
    low = [tails[y][12:16] + tails[2 + y][12:16] + tails[4 + y][12:16] + tails[6 + y][12:16] for y in range(2)]
    low = jnp.concatenate(low, axis=0).astype(bf16)
    for i in range(4):
        up = jnp.concatenate([parts_ref[peers[2 * i], 0:32, :], parts_ref[peers[2 * i + 1], 0:32, :]] * 4, axis=0)
        tail = jnp.where(upper, tails[2 * i + 1], tails[2 * i])
        adapter = dot(low, up, NN)
        adapter = adapter[0:4] + adapter[4:8]
        query = tail[0:4] + tail[4:8] + tail[8:12] + adapter_scale * adapter
        for j in range(2):
            head = query[:, 128 * j : 128 * j + 128]
            mean = jnp.mean(head * head, axis=-1, keepdims=True)
            at = 8 * i + 4 * j
            queries[at : at + 4, :] = head * lax.rsqrt(mean + norm_epsilon) * gain
    normed = queries[...].astype(bf16)
    span = keys_ref.shape[1]
    fresh_k[...] = jnp.zeros_like(fresh_k)
    fresh_v[...] = jnp.zeros_like(fresh_v)
    for i in range(2):
        fresh_k[2 * i : 2 * i + 2, :] = new_keys_ref[i].astype(f32)
        fresh_v[2 * i : 2 * i + 2, :] = new_values_ref[i].astype(f32)
    scale = 128 ** (-0.5)
    first = iota((32, span), 0) % 4 < 2
    scores = jnp.where(first, dot(normed, keys_ref[0], NT), dot(normed, keys_ref[1], NT)) * scale
    limit = jnp.where(first, lengths_ref[0], lengths_ref[1])
    valid = iota((32, span), 1) + f * span < limit
    scores = jnp.where(valid, scores, masked_score)
    line, place = iota((32, 128), 0), iota((32, 128), 1)
    fresh = dot(normed, fresh_k[...].astype(bf16), NT) * scale
    fresh_valid = (place // 2 == (line % 4) // 2) & (place % 2 <= line % 2) & (f == 0)
    fresh = jnp.where(fresh_valid, fresh, masked_score)
    top = jnp.maximum(jnp.max(scores, axis=-1, keepdims=True), jnp.max(fresh, axis=-1, keepdims=True))
    weights = jnp.where(valid, jnp.exp(scores - top), 0.0)
    fresh_weights = jnp.where(fresh_valid, jnp.exp(fresh - top), 0.0)
    total = jnp.sum(weights, axis=-1, keepdims=True) + jnp.sum(fresh_weights, axis=-1, keepdims=True)
    mixed = (
        dot(jnp.where(first, weights, 0.0).astype(bf16), values_ref[0], NN)
        + dot(jnp.where(first, 0.0, weights).astype(bf16), values_ref[1], NN)
        + dot(fresh_weights.astype(bf16), fresh_v[...].astype(bf16), NN)
    )
    stats = jnp.where(iota((32, 128), 1) < 64, top, total)
    for peer, i in enumerate(fsdp_order):
        out_ref[peer, 0:8, :] = mixed[8 * i : 8 * i + 8]
        out_ref[peer, 8:16, :] = stats[8 * i : 8 * i + 8]


def merge(parts_ref, out_ref):
    tops = [parts_ref[i, 8:16, 0:1] for i in range(4)]
    top = jnp.maximum(jnp.maximum(tops[0], tops[1]), jnp.maximum(tops[2], tops[3]))
    total = jnp.zeros((8, 1), f32)
    mixed = jnp.zeros((8, 128), f32)
    for i in range(4):
        scale = jnp.exp(tops[i] - top)
        total += scale * parts_ref[i, 8:16, 64:65]
        mixed += scale * parts_ref[i, 0:8, :]
    result = mixed / total
    for i in range(2):
        for j in range(2):
            out_ref[i, :, 128 * j : 128 * j + 128] = result[4 * j + 2 * i : 4 * j + 2 * i + 2].astype(bf16)


room = pltpu.CompilerParams(vmem_limit_bytes=8 * 2**20)


def exchange(x, axis, order):
    return lax.all_to_all(x, axis, 0, 0, axis_index_groups=[list(order)])


def whole(n):
    return [pl.BlockSpec(memory_space=pltpu.VMEM)] * n


def hbm(n):
    return [pl.BlockSpec(memory_space=pltpu.HBM)] * n


def far(x):
    return pltpu.with_memory_space_constraint(x, pltpu.HBM)


def on_device(
    hidden_in,
    frozen_query_matrix,
    factor_down,
    factor_up,
    query_gain,
    key_cache,
    value_cache,
    new_keys,
    new_values,
    cache_lengths,
):
    packed = pl.pallas_call(
        pack_factors,
        out_shape=jax.ShapeDtypeStruct((8, 16, 384), bf16),
        in_specs=hbm(2),
        out_specs=whole(1)[0],
        scratch_shapes=[
            pltpu.VMEM((16, 320), bf16),
            pltpu.VMEM((4, 256), bf16),
            pltpu.VMEM((16, 128), f32),
            pltpu.SemaphoreType.DMA((2,)),
        ],
        compiler_params=room,
        name="pack_factors",
    )(far(factor_down.T), far(factor_up))
    factors = exchange(packed, "z", z_order)
    other = lax.ppermute(hidden_in, "ylo", ((0, 1), (1, 0)))
    terms, keys, values = pl.pallas_call(
        project,
        out_shape=(
            jax.ShapeDtypeStruct((16, 256), f32),
            pltpu.VMEM(key_cache.shape, bf16),
            pltpu.VMEM(value_cache.shape, bf16),
        ),
        in_specs=hbm(4),
        out_specs=tuple(whole(3)),
        scratch_shapes=[
            pltpu.VMEM((2, 2, 5120), bf16),
            pltpu.VMEM((5120, 256), bf16),
            pltpu.SemaphoreType.DMA((4,)),
        ],
        compiler_params=room,
        cost_estimate=pl.CostEstimate(flops=2 * 4 * 5120 * 256, bytes_accessed=8 * 2**20, transcendentals=0),
        name="project",
    )(far(hidden_in), far(frozen_query_matrix), far(key_cache), far(value_cache))
    aligned = pl.pallas_call(
        align,
        out_shape=jax.ShapeDtypeStruct((8, 8 * 384), bf16),
        in_specs=whole(2),
        out_specs=whole(1)[0],
        scratch_shapes=[pltpu.VMEM((8, 5120), f32)],
        compiler_params=room,
        name="align",
    )(hidden_in, other)
    sent = pl.pallas_call(
        pack_queries,
        out_shape=jax.ShapeDtypeStruct((8, 48, 256), bf16),
        in_specs=whole(3),
        out_specs=whole(1)[0],
        scratch_shapes=[pltpu.VMEM((16, 8 * 384), bf16), pltpu.VMEM((128, 256), bf16)],
        compiler_params=room,
        name="pack_queries",
    )(aligned, terms, factors)
    parts = exchange(sent, ("fsdp", "ylo"), y_order)
    partial = pl.pallas_call(
        attend,
        out_shape=jax.ShapeDtypeStruct((4, 16, 128), f32),
        in_specs=whole(6) + [pl.BlockSpec(memory_space=pltpu.SMEM)],
        out_specs=whole(1)[0],
        scratch_shapes=[pltpu.VMEM((32, 128), f32)] + [pltpu.VMEM((128, 128), f32)] * 2,
        compiler_params=room,
        name="attend",
    )(parts, query_gain.reshape(1, 128), keys, values, new_keys, new_values, cache_lengths)
    partial = exchange(partial, "fsdp", fsdp_order)
    return pl.pallas_call(
        merge,
        out_shape=jax.ShapeDtypeStruct((2, 2, 256), bf16),
        in_specs=whole(1),
        out_specs=whole(1)[0],
        compiler_params=room,
        name="merge",
    )(partial)


def solution(mesh):
    rep = ("z", "ylo")
    lines = mesh.devices.reshape(mesh.devices.shape[0] // 2, 2, *mesh.devices.shape[1:])
    lines = jax.sharding.Mesh(lines, rep + mesh.axis_names[1:])
    placed = (
        P(rep, None, None),
        P(None, ("tp", "fsdp")),
        P(rep, None),
        P(rep, ("tp", "fsdp")),
        P(),
        P(rep, "fsdp", "tp"),
        P(rep, "fsdp", "tp"),
        P(rep, None, "tp"),
        P(rep, None, "tp"),
        P(rep),
    )
    return jax.shard_map(
        on_device,
        mesh=lines,
        in_specs=placed,
        out_specs=P(rep, None, ("tp", "fsdp")),
        check_vma=False,
    )
```

```python
import jax
import jax.numpy as jnp
from jax import lax
from jax.experimental import pallas as pl
from jax.experimental.pallas import tpu as pltpu
from jax.sharding import PartitionSpec as P

adapter_scale = 2.0
norm_epsilon = 1e-06
masked_score = -1e30

z_order = (6, 7, 0, 1, 2, 3, 4, 5)
y_order = (5, 6, 7, 0, 1, 2, 3, 4)
fsdp_order = (2, 3, 0, 1)

NT = (((1,), (1,)), ((), ()))
NN = (((1,), (0,)), ((), ()))
f32, bf16 = jnp.float32, jnp.bfloat16


def dot(a, b, dims):
    return lax.dot_general(a, b, dims, preferred_element_type=f32)


def iota(shape, axis):
    return lax.broadcasted_iota(jnp.int32, shape, axis)


def split3(x):
    hi = x.astype(bf16)
    rest = x - hi.astype(f32)
    mid = rest.astype(bf16)
    lo = (rest - mid.astype(f32)).astype(bf16)
    return hi, mid, lo


def pack_factors(down_hbm, up_hbm, out_ref, down_ref, up_ref, rows_ref, sems):
    start = pl.multiple_of(16 * lax.axis_index("fsdp"), 16)
    down_copy = pltpu.make_async_copy(down_hbm.at[pl.ds(start, 16), :], down_ref, sems.at[0])
    up_copy = pltpu.make_async_copy(up_hbm, up_ref, sems.at[1])
    down_copy.start()
    up_copy.start()
    up_copy.wait()
    up = up_ref[...].astype(f32)
    for i in range(2):
        half = up[:, 128 * i : 128 * i + 128]
        rows_ref[8 * i : 8 * i + 4, :] = pltpu.roll(half, 64, 1)
        rows_ref[8 * i + 4 : 8 * i + 8, :] = half
    down_copy.wait()
    columns = down_ref[...].astype(f32)
    last = jnp.concatenate([columns[:, 256:], jnp.zeros((16, 64), f32)], axis=1)
    last = jnp.where(iota((16, 128), 1) < 64, last, rows_ref[...])
    whole = jnp.concatenate([columns[:, :256], last], axis=1).astype(bf16)
    for peer in range(8):
        out_ref[peer] = whole


def project(hidden_hbm, frozen_hbm, keys_hbm, values_hbm, terms_ref, keys_ref, values_ref, hidden_ref, frozen_ref, sems):
    copies = [
        pltpu.make_async_copy(source, target, sems.at[i])
        for i, (source, target) in enumerate(
            (
                (hidden_hbm, hidden_ref),
                (frozen_hbm, frozen_ref),
                (keys_hbm, keys_ref),
                (values_hbm, values_ref),
            )
        )
    ]
    for copy in copies:
        copy.start()
    copies[0].wait()
    tokens = jnp.concatenate([hidden_ref[0].astype(f32), hidden_ref[1].astype(f32)], axis=0)
    copies[1].wait()
    terms = [t.astype(f32) for t in split3(dot(tokens.astype(bf16), frozen_ref[...], NN))]
    terms_ref[...] = jnp.concatenate(terms + [jnp.zeros((4, 256), f32)], axis=0)
    copies[2].wait()
    copies[3].wait()


def align(hidden_ref, other_ref, out_ref, tokens):
    upper = lax.axis_index("ylo") == 1
    for i in range(2):
        tokens[2 * i : 2 * i + 2, :] = hidden_ref[i].astype(f32)
        tokens[4 + 2 * i : 6 + 2 * i, :] = other_ref[i].astype(f32)
    low = iota((8, 128), 1) < 64
    for peer, z in enumerate(z_order):
        tiles = [tokens[:, 640 * z + 128 * i : 640 * z + 128 * i + 128] for i in range(5)]
        turned = [pltpu.roll(tile, 64, 1) for tile in tiles[2:]] + [jnp.zeros((8, 128), f32)]
        for i in range(3):
            shifted = jnp.where(low, turned[i], turned[i + 1])
            plain = tiles[i] if i < 2 else jnp.where(low, tiles[2], 0.0)
            at = 384 * peer + 128 * i
            out_ref[:, at : at + 128] = jnp.where(upper, shifted, plain).astype(bf16)


def pack_queries(tokens_ref, terms_ref, factors_ref, out_ref, columns, spread):
    f, ylo = lax.axis_index("fsdp"), lax.axis_index("ylo")
    low_half = iota((16, 128), 1) < 64
    here = iota((16, 256), 1) // 64 == iota((16, 256), 0) // 4
    for z in range(8):
        columns[:, 384 * z : 384 * z + 384] = factors_ref[z]
        last = factors_ref[z, :, 256:384].astype(f32)
        rows = jnp.where(low_half, pltpu.roll(last, 64, 1), last)
        rows = jnp.where(here, jnp.concatenate([rows, rows], axis=1), 0.0)
        spread[16 * z : 16 * z + 16, :] = rows.astype(bf16)
    low = dot(tokens_ref[...], columns[...], NT)
    line, place = iota((32, 128), 0), iota((32, 128), 1)
    pick = jnp.zeros((32, 128), jnp.bool_)
    for peer, z in enumerate(z_order):
        pick |= (place // 16 == peer) & (line // 4 == z) & (place % 4 == line % 4)
    pick = pick.astype(f32).astype(bf16)
    up = dot(pick, spread[...], NN).astype(bf16)
    rank = iota((16, 256), 0) + 16 * f
    rank = 32 * (rank // 4 % 2) + 4 * (rank // 8) + rank % 4
    lanes = jnp.zeros((8, 256), f32)
    for i, term in enumerate(split3(low)):
        put = (iota((16, 256), 1) == rank + 64 * i).astype(f32).astype(bf16)
        lanes += dot(term, put, NN)
    tails = []
    for y in range(2):
        part = jnp.where(ylo == y, lanes[0:4], lanes[4:8])
        tails.append(jnp.concatenate([terms_ref[0:12, :], part], axis=0).astype(bf16))
    for peer, y in enumerate(y_order):
        out_ref[peer, 0:32, :] = up
        out_ref[peer, 32:48, :] = tails[y % 2]


def attend(parts_ref, gain_ref, keys_ref, values_ref, new_keys_ref, new_values_ref, lengths_ref, out_ref, queries, fresh_k, fresh_v):
    f = lax.axis_index("fsdp")
    upper = lax.axis_index("ylo") == 1
    peers = [y_order.index(y) for y in range(8)]
    tails = [parts_ref[i, 32:48, :].astype(f32) for i in peers]
    low = [tails[y][12:16] + tails[2 + y][12:16] + tails[4 + y][12:16] + tails[6 + y][12:16] for y in range(2)]
    low = jnp.concatenate(low, axis=0)
    low = jnp.concatenate([low[:, :128], low[:, 128:]], axis=0).astype(bf16)
    for i in range(4):
        up = jnp.concatenate([parts_ref[peers[2 * i], 0:32, :], parts_ref[peers[2 * i + 1], 0:32, :]] * 2, axis=0)
        tail = jnp.where(upper, tails[2 * i + 1], tails[2 * i])
        adapter = dot(low, up, NN)
        adapter = adapter[0:8] + adapter[8:16]
        adapter = adapter[0:4] + adapter[4:8]
        query = tail[0:4] + tail[4:8] + tail[8:12] + adapter_scale * adapter
        for j in range(2):
            at = 8 * i + 4 * j
            queries[at : at + 4, :] = query[:, 128 * j : 128 * j + 128]
    query = queries[...]
    mean = jnp.mean(query * query, axis=-1, keepdims=True)
    normed = (query * lax.rsqrt(mean + norm_epsilon) * gain_ref[...]).astype(bf16)
    span = keys_ref.shape[1]
    fresh_k[...] = jnp.zeros_like(fresh_k)
    fresh_v[...] = jnp.zeros_like(fresh_v)
    for i in range(2):
        fresh_k[2 * i : 2 * i + 2, :] = new_keys_ref[i].astype(f32)
        fresh_v[2 * i : 2 * i + 2, :] = new_values_ref[i].astype(f32)
    scale = 128 ** (-0.5)
    first = iota((32, 128), 0) % 4 < 2
    nothing = jnp.zeros_like(normed)
    both = jnp.concatenate([jnp.where(first, normed, nothing), jnp.where(first, nothing, normed)], axis=1)
    scores = dot(both, jnp.concatenate([keys_ref[0], keys_ref[1]], axis=1), NT) * scale
    lengths = lengths_ref[...]
    limit = jnp.where(iota((32, 1), 0) % 4 < 2, lengths[:, 0:1], lengths[:, 1:2]) - f * span
    scores = jnp.where(iota((32, span), 1) < limit, scores, masked_score)
    line, place = iota((32, 16), 0), iota((32, 16), 1)
    fresh = dot(normed, fresh_k[...].astype(bf16), NT) * scale
    fresh_valid = (place // 2 == (line % 4) // 2) & (place % 2 <= line % 2) & (f == 0)
    fresh = jnp.where(fresh_valid, fresh, masked_score)
    top = jnp.maximum(jnp.max(scores, axis=-1, keepdims=True), jnp.max(fresh, axis=-1, keepdims=True))
    weights = jnp.exp(scores - top)
    fresh_weights = jnp.exp(fresh - top)
    total = jnp.sum(weights, axis=-1, keepdims=True) + jnp.sum(fresh_weights, axis=-1, keepdims=True)
    mixed = dot(weights.astype(bf16), jnp.concatenate([values_ref[0], values_ref[1]], axis=1), NN)
    mixed = jnp.where(first, mixed[:, :128], mixed[:, 128:])
    mixed += dot(fresh_weights.astype(bf16), fresh_v[...].astype(bf16), NN)
    tops, totals = jnp.broadcast_to(top, (32, 128)), jnp.broadcast_to(total, (32, 128))
    for peer, i in enumerate(fsdp_order):
        out_ref[peer, 0:8, :] = mixed[8 * i : 8 * i + 8]
        out_ref[peer, 8:16, :] = tops[8 * i : 8 * i + 8]
        out_ref[peer, 16:24, :] = totals[8 * i : 8 * i + 8]


def merge(parts_ref, out_ref):
    tops = [parts_ref[i, 8:16, :] for i in range(4)]
    top = jnp.maximum(jnp.maximum(tops[0], tops[1]), jnp.maximum(tops[2], tops[3]))
    total = jnp.zeros((8, 128), f32)
    mixed = jnp.zeros((8, 128), f32)
    for i in range(4):
        scale = jnp.exp(tops[i] - top)
        total += scale * parts_ref[i, 16:24, :]
        mixed += scale * parts_ref[i, 0:8, :]
    result = mixed / total
    for i in range(2):
        for j in range(2):
            out_ref[i, :, 128 * j : 128 * j + 128] = result[4 * j + 2 * i : 4 * j + 2 * i + 2].astype(bf16)


room = pltpu.CompilerParams(vmem_limit_bytes=8 * 2**20)


def exchange(x, axis, order):
    return lax.all_to_all(x, axis, 0, 0, axis_index_groups=[list(order)])


def whole(n):
    return [pl.BlockSpec(memory_space=pltpu.VMEM)] * n


def hbm(n):
    return [pl.BlockSpec(memory_space=pltpu.HBM)] * n


def far(x):
    return pltpu.with_memory_space_constraint(x, pltpu.HBM)


def on_device(
    hidden_in,
    frozen_query_matrix,
    factor_down,
    factor_up,
    query_gain,
    key_cache,
    value_cache,
    new_keys,
    new_values,
    cache_lengths,
):
    packed = pl.pallas_call(
        pack_factors,
        out_shape=jax.ShapeDtypeStruct((8, 16, 384), bf16),
        in_specs=hbm(2),
        out_specs=whole(1)[0],
        scratch_shapes=[
            pltpu.VMEM((16, 320), bf16),
            pltpu.VMEM((4, 256), bf16),
            pltpu.VMEM((16, 128), f32),
            pltpu.SemaphoreType.DMA((2,)),
        ],
        compiler_params=room,
        name="pack_factors",
    )(far(factor_down.T), far(factor_up))
    factors = exchange(packed, "z", z_order)
    other = lax.ppermute(hidden_in, "ylo", ((0, 1), (1, 0)))
    terms, keys, values = pl.pallas_call(
        project,
        out_shape=(
            jax.ShapeDtypeStruct((16, 256), f32),
            pltpu.VMEM(key_cache.shape, bf16),
            pltpu.VMEM(value_cache.shape, bf16),
        ),
        in_specs=hbm(4),
        out_specs=tuple(whole(3)),
        scratch_shapes=[
            pltpu.VMEM((2, 2, 5120), bf16),
            pltpu.VMEM((5120, 256), bf16),
            pltpu.SemaphoreType.DMA((4,)),
        ],
        compiler_params=room,
        cost_estimate=pl.CostEstimate(flops=2 * 4 * 5120 * 256, bytes_accessed=8 * 2**20, transcendentals=0),
        name="project",
    )(far(hidden_in), far(frozen_query_matrix), far(key_cache), far(value_cache))
    aligned = pl.pallas_call(
        align,
        out_shape=jax.ShapeDtypeStruct((8, 8 * 384), bf16),
        in_specs=whole(2),
        out_specs=whole(1)[0],
        scratch_shapes=[pltpu.VMEM((8, 5120), f32)],
        compiler_params=room,
        name="align",
    )(hidden_in, other)
    sent = pl.pallas_call(
        pack_queries,
        out_shape=jax.ShapeDtypeStruct((8, 48, 256), bf16),
        in_specs=whole(3),
        out_specs=whole(1)[0],
        scratch_shapes=[pltpu.VMEM((16, 8 * 384), bf16), pltpu.VMEM((128, 256), bf16)],
        compiler_params=room,
        name="pack_queries",
    )(aligned, terms, factors)
    parts = exchange(sent, ("fsdp", "ylo"), y_order)
    partial = pl.pallas_call(
        attend,
        out_shape=jax.ShapeDtypeStruct((4, 24, 128), f32),
        in_specs=whole(7),
        out_specs=whole(1)[0],
        scratch_shapes=[pltpu.VMEM((32, 128), f32)] + [pltpu.VMEM((16, 128), f32)] * 2,
        compiler_params=room,
        name="attend",
    )(parts, query_gain.reshape(1, 128), keys, values, new_keys, new_values, cache_lengths.reshape(1, 2))
    partial = exchange(partial, "fsdp", fsdp_order)
    return pl.pallas_call(
        merge,
        out_shape=jax.ShapeDtypeStruct((2, 2, 256), bf16),
        in_specs=whole(1),
        out_specs=whole(1)[0],
        compiler_params=room,
        name="merge",
    )(partial)


def solution(mesh):
    rep = ("z", "ylo")
    lines = mesh.devices.reshape(mesh.devices.shape[0] // 2, 2, *mesh.devices.shape[1:])
    lines = jax.sharding.Mesh(lines, rep + mesh.axis_names[1:])
    placed = (
        P(rep, None, None),
        P(None, ("tp", "fsdp")),
        P(rep, None),
        P(rep, ("tp", "fsdp")),
        P(),
        P(rep, "fsdp", "tp"),
        P(rep, "fsdp", "tp"),
        P(rep, None, "tp"),
        P(rep, None, "tp"),
        P(rep),
    )
    return jax.shard_map(
        on_device,
        mesh=lines,
        in_specs=placed,
        out_specs=P(rep, None, ("tp", "fsdp")),
        check_vma=False,
    )
```

```python
import jax
import jax.numpy as jnp
from jax import lax
from jax.experimental import pallas as pl
from jax.experimental.pallas import tpu as pltpu
from jax.sharding import PartitionSpec as P

adapter_scale = 2.0
norm_epsilon = 1e-06
masked_score = -1e30

z_order = (6, 7, 0, 1, 2, 3, 4, 5)
y_order = (5, 6, 7, 0, 1, 2, 3, 4)
fsdp_order = (2, 3, 0, 1)

NT = (((1,), (1,)), ((), ()))
NN = (((1,), (0,)), ((), ()))
f32, bf16 = jnp.float32, jnp.bfloat16


def dot(a, b, dims):
    return lax.dot_general(a, b, dims, preferred_element_type=f32)


def iota(shape, axis):
    return lax.broadcasted_iota(jnp.int32, shape, axis)


def split3(x):
    hi = x.astype(bf16)
    rest = x - hi.astype(f32)
    mid = rest.astype(bf16)
    lo = (rest - mid.astype(f32)).astype(bf16)
    return hi, mid, lo


def pack_factors(down_hbm, up_hbm, hidden_hbm, out_hbm, own_ref, other_ref, down_ref, up_ref, hidden_ref, rows_ref, packed, tokens, sems):
    down_copy = pltpu.make_async_copy(down_hbm, down_ref, sems.at[0])
    up_copy = pltpu.make_async_copy(up_hbm, up_ref, sems.at[1])
    hidden_copy = pltpu.make_async_copy(hidden_hbm, hidden_ref, sems.at[2])
    down_copy.start()
    up_copy.start()
    hidden_copy.start()
    up_copy.wait()
    up = up_ref[...].astype(f32)
    for i in range(2):
        half = up[:, 128 * i : 128 * i + 128]
        rows_ref[8 * i : 8 * i + 4, :] = pltpu.roll(half, 64, 1)
        rows_ref[8 * i + 4 : 8 * i + 8, :] = half
    down_copy.wait()
    start = pl.multiple_of(16 * lax.axis_index("fsdp"), 16)
    columns = down_ref[pl.ds(start, 16), :].astype(f32)
    last = jnp.concatenate([columns[:, 256:], jnp.zeros((16, 64), f32)], axis=1)
    last = jnp.where(iota((16, 128), 1) < 64, last, rows_ref[...])
    packed[...] = jnp.concatenate([columns[:, :256], last], axis=1).astype(bf16)
    out_copies = [pltpu.make_async_copy(packed, out_hbm.at[peer], sems.at[3 + peer]) for peer in range(8)]
    for copy in out_copies:
        copy.start()
    hidden_copy.wait()
    upper = lax.axis_index("ylo") == 1
    for i in range(2):
        tokens[2 * i : 2 * i + 2, :] = hidden_ref[i].astype(f32)
    low = iota((4, 128), 1) < 64
    for peer, z in enumerate(z_order):
        tiles = [tokens[:, 640 * z + 128 * i : 640 * z + 128 * i + 128] for i in range(5)]
        turned = [pltpu.roll(tile, 64, 1) for tile in tiles[2:]] + [jnp.zeros((4, 128), f32)]
        for i in range(3):
            shifted = jnp.where(low, turned[i], turned[i + 1])
            plain = tiles[i] if i < 2 else jnp.where(low, tiles[2], 0.0)
            at = 384 * peer + 128 * i
            own_ref[:, at : at + 128] = jnp.where(upper, shifted, plain).astype(bf16)
            other_ref[:, at : at + 128] = jnp.where(upper, plain, shifted).astype(bf16)
    for copy in out_copies:
        copy.wait()


def project(hidden_hbm, frozen_hbm, terms_ref, hidden_ref, frozen_ref, sems):
    copies = [
        pltpu.make_async_copy(source, target, sems.at[i])
        for i, (source, target) in enumerate(
            (
                (hidden_hbm, hidden_ref),
                (frozen_hbm, frozen_ref),
            )
        )
    ]
    for copy in copies:
        copy.start()
    copies[0].wait()
    tokens = jnp.concatenate([hidden_ref[0].astype(f32), hidden_ref[1].astype(f32)], axis=0)
    copies[1].wait()
    terms = [t.astype(f32) for t in split3(dot(tokens.astype(bf16), frozen_ref[...], NN))]
    terms_ref[...] = jnp.concatenate(terms + [jnp.zeros((4, 256), f32)], axis=0)


def pack_queries(own_ref, other_ref, terms_ref, factors_ref, out_ref, columns, spread):
    f, ylo = lax.axis_index("fsdp"), lax.axis_index("ylo")
    low_half = iota((16, 128), 1) < 64
    here = iota((16, 256), 1) // 64 == iota((16, 256), 0) // 4
    for z in range(8):
        columns[:, 384 * z : 384 * z + 384] = factors_ref[z]
        last = factors_ref[z, :, 256:384].astype(f32)
        rows = jnp.where(low_half, pltpu.roll(last, 64, 1), last)
        rows = jnp.where(here, jnp.concatenate([rows, rows], axis=1), 0.0)
        spread[16 * z : 16 * z + 16, :] = rows.astype(bf16)
    tokens = jnp.concatenate([own_ref[...].astype(f32), other_ref[...].astype(f32)], axis=0).astype(bf16)
    low = dot(tokens, columns[...], NT)
    line, place = iota((32, 128), 0), iota((32, 128), 1)
    pick = jnp.zeros((32, 128), jnp.bool_)
    for peer, z in enumerate(z_order):
        pick |= (place // 16 == peer) & (line // 4 == z) & (place % 4 == line % 4)
    pick = pick.astype(f32).astype(bf16)
    up = dot(pick, spread[...], NN).astype(bf16)
    rank = iota((16, 256), 0) + 16 * f
    rank = 32 * (rank // 4 % 2) + 4 * (rank // 8) + rank % 4
    lanes = jnp.zeros((8, 256), f32)
    for i, term in enumerate(split3(low)):
        put = (iota((16, 256), 1) == rank + 64 * i).astype(f32).astype(bf16)
        lanes += dot(term, put, NN)
    tails = []
    for y in range(2):
        part = jnp.where(ylo == y, lanes[0:4], lanes[4:8])
        tails.append(jnp.concatenate([terms_ref[0:12, :], part], axis=0).astype(bf16))
    for peer, y in enumerate(y_order):
        out_ref[peer, 0:32, :] = up
        out_ref[peer, 32:48, :] = tails[y % 2]


def attend(parts_ref, gain_ref, keys_ref, values_ref, new_keys_ref, new_values_ref, lengths_ref, out_ref, queries, fresh_k, fresh_v):
    f = lax.axis_index("fsdp")
    upper = lax.axis_index("ylo") == 1
    peers = [y_order.index(y) for y in range(8)]
    tails = [parts_ref[i, 32:48, :].astype(f32) for i in peers]
    low = [tails[y][12:16] + tails[2 + y][12:16] + tails[4 + y][12:16] + tails[6 + y][12:16] for y in range(2)]
    low = jnp.concatenate(low, axis=0)
    low = jnp.concatenate([low[:, :128], low[:, 128:]], axis=0).astype(bf16)
    for i in range(4):
        up = jnp.concatenate([parts_ref[peers[2 * i], 0:32, :], parts_ref[peers[2 * i + 1], 0:32, :]] * 2, axis=0)
        tail = jnp.where(upper, tails[2 * i + 1], tails[2 * i])
        adapter = dot(low, up, NN)
        adapter = adapter[0:8] + adapter[8:16]
        adapter = adapter[0:4] + adapter[4:8]
        query = tail[0:4] + tail[4:8] + tail[8:12] + adapter_scale * adapter
        for j in range(2):
            at = 8 * i + 4 * j
            queries[at : at + 4, :] = query[:, 128 * j : 128 * j + 128]
    query = queries[...]
    mean = jnp.mean(query * query, axis=-1, keepdims=True)
    normed = (query * lax.rsqrt(mean + norm_epsilon) * gain_ref[...]).astype(bf16)
    span = keys_ref.shape[1]
    fresh_k[...] = jnp.zeros_like(fresh_k)
    fresh_v[...] = jnp.zeros_like(fresh_v)
    for i in range(2):
        fresh_k[2 * i : 2 * i + 2, :] = new_keys_ref[i].astype(f32)
        fresh_v[2 * i : 2 * i + 2, :] = new_values_ref[i].astype(f32)
    scale = 128 ** (-0.5)
    first = iota((32, 128), 0) % 4 < 2
    nothing = jnp.zeros_like(normed)
    both = jnp.concatenate([jnp.where(first, normed, nothing), jnp.where(first, nothing, normed)], axis=1)
    scores = dot(both, jnp.concatenate([keys_ref[0], keys_ref[1]], axis=1), NT) * scale
    lengths = lengths_ref[...]
    limit = jnp.where(iota((32, 1), 0) % 4 < 2, lengths[:, 0:1], lengths[:, 1:2]) - f * span
    scores = jnp.where(iota((32, span), 1) < limit, scores, masked_score)
    line, place = iota((32, 16), 0), iota((32, 16), 1)
    fresh = dot(normed, fresh_k[...].astype(bf16), NT) * scale
    fresh_valid = (place // 2 == (line % 4) // 2) & (place % 2 <= line % 2) & (f == 0)
    fresh = jnp.where(fresh_valid, fresh, masked_score)
    top = jnp.maximum(jnp.max(scores, axis=-1, keepdims=True), jnp.max(fresh, axis=-1, keepdims=True))
    weights = jnp.exp(scores - top)
    fresh_weights = jnp.exp(fresh - top)
    total = jnp.sum(weights, axis=-1, keepdims=True) + jnp.sum(fresh_weights, axis=-1, keepdims=True)
    mixed = dot(weights.astype(bf16), jnp.concatenate([values_ref[0], values_ref[1]], axis=1), NN)
    mixed = jnp.where(first, mixed[:, :128], mixed[:, 128:])
    mixed += dot(fresh_weights.astype(bf16), fresh_v[...].astype(bf16), NN)
    tops, totals = jnp.broadcast_to(top, (32, 128)), jnp.broadcast_to(total, (32, 128))
    for peer, i in enumerate(fsdp_order):
        out_ref[peer, 0:8, :] = mixed[8 * i : 8 * i + 8]
        out_ref[peer, 8:16, :] = tops[8 * i : 8 * i + 8]
        out_ref[peer, 16:24, :] = totals[8 * i : 8 * i + 8]


def merge(parts_ref, out_ref):
    tops = [parts_ref[i, 8:16, :] for i in range(4)]
    top = jnp.maximum(jnp.maximum(tops[0], tops[1]), jnp.maximum(tops[2], tops[3]))
    total = jnp.zeros((8, 128), f32)
    mixed = jnp.zeros((8, 128), f32)
    for i in range(4):
        scale = jnp.exp(tops[i] - top)
        total += scale * parts_ref[i, 16:24, :]
        mixed += scale * parts_ref[i, 0:8, :]
    result = mixed / total
    for i in range(2):
        for j in range(2):
            out_ref[i, :, 128 * j : 128 * j + 128] = result[4 * j + 2 * i : 4 * j + 2 * i + 2].astype(bf16)


room = pltpu.CompilerParams(vmem_limit_bytes=8 * 2**20)


def exchange(x, axis, order):
    return lax.all_to_all(x, axis, 0, 0, axis_index_groups=[list(order)])


def whole(n):
    return [pl.BlockSpec(memory_space=pltpu.VMEM)] * n


def hbm(n):
    return [pl.BlockSpec(memory_space=pltpu.HBM)] * n


def far(x):
    return pltpu.with_memory_space_constraint(x, pltpu.HBM)


def on_device(
    hidden_in,
    frozen_query_matrix,
    factor_down,
    factor_up,
    query_gain,
    key_cache,
    value_cache,
    new_keys,
    new_values,
    cache_lengths,
):
    packed, own, lent = pl.pallas_call(
        pack_factors,
        out_shape=(
            jax.ShapeDtypeStruct((8, 16, 384), bf16),
            pltpu.VMEM((4, 8 * 384), bf16),
            jax.ShapeDtypeStruct((4, 8 * 384), bf16),
        ),
        in_specs=hbm(3),
        out_specs=(hbm(1)[0], *whole(2)),
        scratch_shapes=[
            pltpu.VMEM((64, 320), bf16),
            pltpu.VMEM((4, 256), bf16),
            pltpu.VMEM((2, 2, 5120), bf16),
            pltpu.VMEM((16, 128), f32),
            pltpu.VMEM((16, 384), bf16),
            pltpu.VMEM((4, 5120), f32),
            pltpu.SemaphoreType.DMA((11,)),
        ],
        compiler_params=room,
        name="pack_factors",
    )(far(factor_down.T), far(factor_up), far(hidden_in))
    factors = exchange(packed, "z", z_order)
    other = lax.ppermute(lent, "ylo", ((0, 1), (1, 0)))
    terms = pl.pallas_call(
        project,
        out_shape=jax.ShapeDtypeStruct((16, 256), f32),
        in_specs=hbm(2),
        out_specs=whole(1)[0],
        scratch_shapes=[
            pltpu.VMEM((2, 2, 5120), bf16),
            pltpu.VMEM((5120, 256), bf16),
            pltpu.SemaphoreType.DMA((2,)),
        ],
        compiler_params=room,
        cost_estimate=pl.CostEstimate(flops=2 * 4 * 5120 * 256, bytes_accessed=8 * 2**20, transcendentals=0),
        name="project",
    )(far(hidden_in), far(frozen_query_matrix))
    sent = pl.pallas_call(
        pack_queries,
        out_shape=jax.ShapeDtypeStruct((8, 48, 256), bf16),
        in_specs=whole(4),
        out_specs=whole(1)[0],
        scratch_shapes=[pltpu.VMEM((16, 8 * 384), bf16), pltpu.VMEM((128, 256), bf16)],
        compiler_params=room,
        name="pack_queries",
    )(own, other, terms, factors)
    parts = exchange(sent, ("fsdp", "ylo"), y_order)
    partial = pl.pallas_call(
        attend,
        out_shape=jax.ShapeDtypeStruct((4, 24, 128), f32),
        in_specs=whole(7),
        out_specs=whole(1)[0],
        scratch_shapes=[pltpu.VMEM((32, 128), f32)] + [pltpu.VMEM((16, 128), f32)] * 2,
        compiler_params=room,
        name="attend",
    )(parts, query_gain.reshape(1, 128), key_cache, value_cache, new_keys, new_values, cache_lengths.reshape(1, 2))
    partial = exchange(partial, "fsdp", fsdp_order)
    return pl.pallas_call(
        merge,
        out_shape=jax.ShapeDtypeStruct((2, 2, 256), bf16),
        in_specs=whole(1),
        out_specs=whole(1)[0],
        compiler_params=room,
        name="merge",
    )(partial)


def solution(mesh):
    rep = ("z", "ylo")
    lines = mesh.devices.reshape(mesh.devices.shape[0] // 2, 2, *mesh.devices.shape[1:])
    lines = jax.sharding.Mesh(lines, rep + mesh.axis_names[1:])
    placed = (
        P(rep, None, None),
        P(None, ("tp", "fsdp")),
        P(rep, None),
        P(rep, ("tp", "fsdp")),
        P(),
        P(rep, "fsdp", "tp"),
        P(rep, "fsdp", "tp"),
        P(rep, None, "tp"),
        P(rep, None, "tp"),
        P(rep),
    )
    return jax.shard_map(
        on_device,
        mesh=lines,
        in_specs=placed,
        out_specs=P(rep, None, ("tp", "fsdp")),
        check_vma=False,
    )
```

```python
import jax
import jax.numpy as jnp
from jax import lax
from jax.experimental import pallas as pl
from jax.experimental.pallas import tpu as pltpu
from jax.sharding import PartitionSpec as P

adapter_scale = 2.0
norm_epsilon = 1e-06
masked_score = -1e30

z_order = (6, 7, 0, 1, 2, 3, 4, 5)
y_order = (5, 1, 0, 2, 3, 4, 6, 7)
fsdp_order = (2, 3, 0, 1)

NT = (((1,), (1,)), ((), ()))
NN = (((1,), (0,)), ((), ()))
f32, bf16 = jnp.float32, jnp.bfloat16


def dot(a, b, dims):
    return lax.dot_general(a, b, dims, preferred_element_type=f32)


def iota(shape, axis):
    return lax.broadcasted_iota(jnp.int32, shape, axis)


def split3(x):
    hi = x.astype(bf16)
    rest = x - hi.astype(f32)
    mid = rest.astype(bf16)
    lo = (rest - mid.astype(f32)).astype(bf16)
    return hi, mid, lo


def pack_factors(down_hbm, up_hbm, hidden_hbm, out_hbm, own_ref, other_ref, down_ref, up_ref, hidden_ref, rows_ref, packed, tokens, sems):
    down_copy = pltpu.make_async_copy(down_hbm, down_ref, sems.at[0])
    up_copy = pltpu.make_async_copy(up_hbm, up_ref, sems.at[1])
    hidden_copy = pltpu.make_async_copy(hidden_hbm, hidden_ref, sems.at[2])
    down_copy.start()
    up_copy.start()
    hidden_copy.start()
    up_copy.wait()
    up = up_ref[...].astype(f32)
    for i in range(2):
        half = up[:, 128 * i : 128 * i + 128]
        rows_ref[8 * i : 8 * i + 4, :] = pltpu.roll(half, 64, 1)
        rows_ref[8 * i + 4 : 8 * i + 8, :] = half
    down_copy.wait()
    start = pl.multiple_of(16 * lax.axis_index("fsdp"), 16)
    columns = down_ref[pl.ds(start, 16), :].astype(f32)
    last = jnp.concatenate([columns[:, 256:], jnp.zeros((16, 64), f32)], axis=1)
    last = jnp.where(iota((16, 128), 1) < 64, last, rows_ref[...])
    packed[...] = jnp.concatenate([columns[:, :256], last], axis=1).astype(bf16)
    out_copies = [pltpu.make_async_copy(packed, out_hbm.at[peer], sems.at[3 + peer]) for peer in range(8)]
    for copy in out_copies:
        copy.start()
    hidden_copy.wait()
    upper = lax.axis_index("ylo") == 1
    for i in range(2):
        tokens[2 * i : 2 * i + 2, :] = hidden_ref[i].astype(f32)
    low = iota((4, 128), 1) < 64
    for peer, z in enumerate(z_order):
        tiles = [tokens[:, 640 * z + 128 * i : 640 * z + 128 * i + 128] for i in range(5)]
        turned = [pltpu.roll(tile, 64, 1) for tile in tiles[2:]] + [jnp.zeros((4, 128), f32)]
        for i in range(3):
            shifted = jnp.where(low, turned[i], turned[i + 1])
            plain = tiles[i] if i < 2 else jnp.where(low, tiles[2], 0.0)
            at = 384 * peer + 128 * i
            own_ref[:, at : at + 128] = jnp.where(upper, shifted, plain).astype(bf16)
            other_ref[:, at : at + 128] = jnp.where(upper, plain, shifted).astype(bf16)
    for copy in out_copies:
        copy.wait()


def project(hidden_hbm, frozen_hbm, terms_ref, hidden_ref, frozen_ref, sems):
    copies = [
        pltpu.make_async_copy(source, target, sems.at[i])
        for i, (source, target) in enumerate(
            (
                (hidden_hbm, hidden_ref),
                (frozen_hbm, frozen_ref),
            )
        )
    ]
    for copy in copies:
        copy.start()
    copies[0].wait()
    tokens = jnp.concatenate([hidden_ref[0].astype(f32), hidden_ref[1].astype(f32)], axis=0)
    copies[1].wait()
    terms = [t.astype(f32) for t in split3(dot(tokens.astype(bf16), frozen_ref[...], NN))]
    terms_ref[...] = jnp.concatenate(terms + [jnp.zeros((4, 256), f32)], axis=0)


def pack_queries(own_ref, other_ref, terms_ref, factors_ref, out_ref, columns, spread):
    f, ylo = lax.axis_index("fsdp"), lax.axis_index("ylo")
    low_half = iota((16, 128), 1) < 64
    here = iota((16, 256), 1) // 64 == iota((16, 256), 0) // 4
    for z in range(8):
        columns[:, 384 * z : 384 * z + 384] = factors_ref[z]
        last = factors_ref[z, :, 256:384].astype(f32)
        rows = jnp.where(low_half, pltpu.roll(last, 64, 1), last)
        rows = jnp.where(here, jnp.concatenate([rows, rows], axis=1), 0.0)
        spread[16 * z : 16 * z + 16, :] = rows.astype(bf16)
    tokens = jnp.concatenate([own_ref[...].astype(f32), other_ref[...].astype(f32)], axis=0).astype(bf16)
    low = dot(tokens, columns[...], NT)
    line, place = iota((32, 128), 0), iota((32, 128), 1)
    pick = jnp.zeros((32, 128), jnp.bool_)
    for peer, z in enumerate(z_order):
        pick |= (place // 16 == peer) & (line // 4 == z) & (place % 4 == line % 4)
    pick = pick.astype(f32).astype(bf16)
    up = dot(pick, spread[...], NN).astype(bf16)
    rank = iota((16, 256), 0) + 16 * f
    rank = 32 * (rank // 4 % 2) + 4 * (rank // 8) + rank % 4
    lanes = jnp.zeros((8, 256), f32)
    for i, term in enumerate(split3(low)):
        put = (iota((16, 256), 1) == rank + 64 * i).astype(f32).astype(bf16)
        lanes += dot(term, put, NN)
    tails = []
    for y in range(2):
        part = jnp.where(ylo == y, lanes[0:4], lanes[4:8])
        tails.append(jnp.concatenate([terms_ref[0:12, :], part], axis=0).astype(bf16))
    for peer, y in enumerate(y_order):
        out_ref[peer, 0:32, :] = up
        out_ref[peer, 32:48, :] = tails[y % 2]


def attend(parts_ref, gain_ref, keys_ref, values_ref, new_keys_ref, new_values_ref, lengths_ref, out_ref, queries, fresh_k, fresh_v):
    f = lax.axis_index("fsdp")
    upper = lax.axis_index("ylo") == 1
    peers = [y_order.index(y) for y in range(8)]
    tails = [parts_ref[i, 32:48, :].astype(f32) for i in peers]
    low = [tails[y][12:16] + tails[2 + y][12:16] + tails[4 + y][12:16] + tails[6 + y][12:16] for y in range(2)]
    low = jnp.concatenate(low, axis=0)
    low = jnp.concatenate([low[:, :128], low[:, 128:]], axis=0).astype(bf16)
    for i in range(4):
        up = jnp.concatenate([parts_ref[peers[2 * i], 0:32, :], parts_ref[peers[2 * i + 1], 0:32, :]] * 2, axis=0)
        tail = jnp.where(upper, tails[2 * i + 1], tails[2 * i])
        adapter = dot(low, up, NN)
        adapter = adapter[0:8] + adapter[8:16]
        adapter = adapter[0:4] + adapter[4:8]
        query = tail[0:4] + tail[4:8] + tail[8:12] + adapter_scale * adapter
        for j in range(2):
            at = 8 * i + 4 * j
            queries[at : at + 4, :] = query[:, 128 * j : 128 * j + 128]
    query = queries[...]
    mean = jnp.mean(query * query, axis=-1, keepdims=True)
    normed = (query * lax.rsqrt(mean + norm_epsilon) * gain_ref[...]).astype(bf16)
    span = keys_ref.shape[1]
    fresh_k[...] = jnp.zeros_like(fresh_k)
    fresh_v[...] = jnp.zeros_like(fresh_v)
    for i in range(2):
        fresh_k[2 * i : 2 * i + 2, :] = new_keys_ref[i].astype(f32)
        fresh_v[2 * i : 2 * i + 2, :] = new_values_ref[i].astype(f32)
    scale = 128 ** (-0.5)
    first = iota((32, 128), 0) % 4 < 2
    nothing = jnp.zeros_like(normed)
    both = jnp.concatenate([jnp.where(first, normed, nothing), jnp.where(first, nothing, normed)], axis=1)
    scores = dot(both, jnp.concatenate([keys_ref[0], keys_ref[1]], axis=1), NT) * scale
    lengths = lengths_ref[...]
    limit = jnp.where(iota((32, 1), 0) % 4 < 2, lengths[:, 0:1], lengths[:, 1:2]) - f * span
    scores = jnp.where(iota((32, span), 1) < limit, scores, masked_score)
    line, place = iota((32, 16), 0), iota((32, 16), 1)
    fresh = dot(normed, fresh_k[...].astype(bf16), NT) * scale
    fresh_valid = (place // 2 == (line % 4) // 2) & (place % 2 <= line % 2) & (f == 0)
    fresh = jnp.where(fresh_valid, fresh, masked_score)
    top = jnp.maximum(jnp.max(scores, axis=-1, keepdims=True), jnp.max(fresh, axis=-1, keepdims=True))
    weights = jnp.exp(scores - top)
    fresh_weights = jnp.exp(fresh - top)
    total = jnp.sum(weights, axis=-1, keepdims=True) + jnp.sum(fresh_weights, axis=-1, keepdims=True)
    mixed = dot(weights.astype(bf16), jnp.concatenate([values_ref[0], values_ref[1]], axis=1), NN)
    mixed = jnp.where(first, mixed[:, :128], mixed[:, 128:])
    mixed += dot(fresh_weights.astype(bf16), fresh_v[...].astype(bf16), NN)
    tops, totals = jnp.broadcast_to(top, (32, 128)), jnp.broadcast_to(total, (32, 128))
    for peer, i in enumerate(fsdp_order):
        out_ref[peer, 0:8, :] = mixed[8 * i : 8 * i + 8]
        out_ref[peer, 8:16, :] = tops[8 * i : 8 * i + 8]
        out_ref[peer, 16:24, :] = totals[8 * i : 8 * i + 8]


def merge(parts_ref, out_ref):
    tops = [parts_ref[i, 8:16, :] for i in range(4)]
    top = jnp.maximum(jnp.maximum(tops[0], tops[1]), jnp.maximum(tops[2], tops[3]))
    total = jnp.zeros((8, 128), f32)
    mixed = jnp.zeros((8, 128), f32)
    for i in range(4):
        scale = jnp.exp(tops[i] - top)
        total += scale * parts_ref[i, 16:24, :]
        mixed += scale * parts_ref[i, 0:8, :]
    result = mixed / total
    for i in range(2):
        for j in range(2):
            out_ref[i, :, 128 * j : 128 * j + 128] = result[4 * j + 2 * i : 4 * j + 2 * i + 2].astype(bf16)


room = pltpu.CompilerParams(vmem_limit_bytes=8 * 2**20)


def exchange(x, axis, order):
    return lax.all_to_all(x, axis, 0, 0, axis_index_groups=[list(order)])


def whole(n):
    return [pl.BlockSpec(memory_space=pltpu.VMEM)] * n


def hbm(n):
    return [pl.BlockSpec(memory_space=pltpu.HBM)] * n


def far(x):
    return pltpu.with_memory_space_constraint(x, pltpu.HBM)


def on_device(
    hidden_in,
    frozen_query_matrix,
    factor_down,
    factor_up,
    query_gain,
    key_cache,
    value_cache,
    new_keys,
    new_values,
    cache_lengths,
):
    packed, own, lent = pl.pallas_call(
        pack_factors,
        out_shape=(
            jax.ShapeDtypeStruct((8, 16, 384), bf16),
            pltpu.VMEM((4, 8 * 384), bf16),
            jax.ShapeDtypeStruct((4, 8 * 384), bf16),
        ),
        in_specs=hbm(3),
        out_specs=(hbm(1)[0], *whole(2)),
        scratch_shapes=[
            pltpu.VMEM((64, 320), bf16),
            pltpu.VMEM((4, 256), bf16),
            pltpu.VMEM((2, 2, 5120), bf16),
            pltpu.VMEM((16, 128), f32),
            pltpu.VMEM((16, 384), bf16),
            pltpu.VMEM((4, 5120), f32),
            pltpu.SemaphoreType.DMA((11,)),
        ],
        compiler_params=room,
        name="pack_factors",
    )(far(factor_down.T), far(factor_up), far(hidden_in))
    factors = exchange(packed, "z", z_order)
    other = lax.ppermute(lent, "ylo", ((0, 1), (1, 0)))
    terms = pl.pallas_call(
        project,
        out_shape=jax.ShapeDtypeStruct((16, 256), f32),
        in_specs=hbm(2),
        out_specs=whole(1)[0],
        scratch_shapes=[
            pltpu.VMEM((2, 2, 5120), bf16),
            pltpu.VMEM((5120, 256), bf16),
            pltpu.SemaphoreType.DMA((2,)),
        ],
        compiler_params=room,
        cost_estimate=pl.CostEstimate(flops=2 * 4 * 5120 * 256, bytes_accessed=8 * 2**20, transcendentals=0),
        name="project",
    )(far(hidden_in), far(frozen_query_matrix))
    sent = pl.pallas_call(
        pack_queries,
        out_shape=jax.ShapeDtypeStruct((8, 48, 256), bf16),
        in_specs=whole(4),
        out_specs=whole(1)[0],
        scratch_shapes=[pltpu.VMEM((16, 8 * 384), bf16), pltpu.VMEM((128, 256), bf16)],
        compiler_params=room,
        name="pack_queries",
    )(own, other, terms, factors)
    parts = exchange(sent, ("fsdp", "ylo"), y_order)
    partial = pl.pallas_call(
        attend,
        out_shape=jax.ShapeDtypeStruct((4, 24, 128), f32),
        in_specs=whole(7),
        out_specs=whole(1)[0],
        scratch_shapes=[pltpu.VMEM((32, 128), f32)] + [pltpu.VMEM((16, 128), f32)] * 2,
        compiler_params=room,
        name="attend",
    )(parts, query_gain.reshape(1, 128), key_cache, value_cache, new_keys, new_values, cache_lengths.reshape(1, 2))
    partial = exchange(partial, "fsdp", fsdp_order)
    return pl.pallas_call(
        merge,
        out_shape=jax.ShapeDtypeStruct((2, 2, 256), bf16),
        in_specs=whole(1),
        out_specs=whole(1)[0],
        compiler_params=room,
        name="merge",
    )(partial)


def solution(mesh):
    rep = ("z", "ylo")
    lines = mesh.devices.reshape(mesh.devices.shape[0] // 2, 2, *mesh.devices.shape[1:])
    lines = jax.sharding.Mesh(lines, rep + mesh.axis_names[1:])
    placed = (
        P(rep, None, None),
        P(None, ("tp", "fsdp")),
        P(rep, None),
        P(rep, ("tp", "fsdp")),
        P(),
        P(rep, "fsdp", "tp"),
        P(rep, "fsdp", "tp"),
        P(rep, None, "tp"),
        P(rep, None, "tp"),
        P(rep),
    )
    return jax.shard_map(
        on_device,
        mesh=lines,
        in_specs=placed,
        out_specs=P(rep, None, ("tp", "fsdp")),
        check_vma=False,
    )
```

```python
import jax
import jax.numpy as jnp
from jax import lax
from jax.experimental import pallas as pl
from jax.experimental.pallas import tpu as pltpu
from jax.sharding import PartitionSpec as P

adapter_scale = 2.0
norm_epsilon = 1e-06
masked_score = -1e30

z_order = (6, 7, 0, 1, 2, 3, 4, 5)
y_order = (5, 1, 0, 2, 3, 4, 6, 7)
fsdp_order = (2, 3, 0, 1)

NT = (((1,), (1,)), ((), ()))
NN = (((1,), (0,)), ((), ()))
f32, bf16 = jnp.float32, jnp.bfloat16


def dot(a, b, dims):
    return lax.dot_general(a, b, dims, preferred_element_type=f32)


def iota(shape, axis):
    return lax.broadcasted_iota(jnp.int32, shape, axis)


def split3(x):
    hi = x.astype(bf16)
    rest = x - hi.astype(f32)
    mid = rest.astype(bf16)
    lo = (rest - mid.astype(f32)).astype(bf16)
    return hi, mid, lo


def pack_factors(down_hbm, up_hbm, hidden_hbm, out_hbm, own_ref, other_ref, down_ref, up_ref, hidden_ref, rows_ref, packed, tokens, sems):
    down_copy = pltpu.make_async_copy(down_hbm, down_ref, sems.at[0])
    up_copy = pltpu.make_async_copy(up_hbm, up_ref, sems.at[1])
    hidden_copy = pltpu.make_async_copy(hidden_hbm, hidden_ref, sems.at[2])
    down_copy.start()
    up_copy.start()
    hidden_copy.start()
    up_copy.wait()
    up = up_ref[...].astype(f32)
    for i in range(2):
        half = up[:, 128 * i : 128 * i + 128]
        rows_ref[8 * i : 8 * i + 4, :] = pltpu.roll(half, 64, 1)
        rows_ref[8 * i + 4 : 8 * i + 8, :] = half
    down_copy.wait()
    start = pl.multiple_of(16 * lax.axis_index("fsdp"), 16)
    columns = down_ref[pl.ds(start, 16), :].astype(f32)
    last = jnp.concatenate([columns[:, 256:], jnp.zeros((16, 64), f32)], axis=1)
    last = jnp.where(iota((16, 128), 1) < 64, last, rows_ref[...])
    packed[...] = jnp.concatenate([columns[:, :256], last], axis=1).astype(bf16)
    out_copies = [pltpu.make_async_copy(packed, out_hbm.at[peer], sems.at[3 + peer]) for peer in range(8)]
    for copy in out_copies:
        copy.start()
    hidden_copy.wait()
    upper = lax.axis_index("ylo") == 1
    for i in range(2):
        tokens[2 * i : 2 * i + 2, :] = hidden_ref[i].astype(f32)
    low = iota((4, 128), 1) < 64
    for peer, z in enumerate(z_order):
        tiles = [tokens[:, 640 * z + 128 * i : 640 * z + 128 * i + 128] for i in range(5)]
        turned = [pltpu.roll(tile, 64, 1) for tile in tiles[2:]] + [jnp.zeros((4, 128), f32)]
        for i in range(3):
            shifted = jnp.where(low, turned[i], turned[i + 1])
            plain = tiles[i] if i < 2 else jnp.where(low, tiles[2], 0.0)
            at = 384 * peer + 128 * i
            own_ref[:, at : at + 128] = jnp.where(upper, shifted, plain).astype(bf16)
            other_ref[:, at : at + 128] = jnp.where(upper, plain, shifted).astype(bf16)
    for copy in out_copies:
        copy.wait()


def project(hidden_hbm, frozen_hbm, terms_ref, pick_ref, put_ref, hidden_ref, frozen_ref, sems):
    copies = [
        pltpu.make_async_copy(source, target, sems.at[i])
        for i, (source, target) in enumerate(
            (
                (hidden_hbm, hidden_ref),
                (frozen_hbm, frozen_ref),
            )
        )
    ]
    for copy in copies:
        copy.start()
    line, place = iota((32, 128), 0), iota((32, 128), 1)
    pick = jnp.zeros((32, 128), jnp.bool_)
    for peer, z in enumerate(z_order):
        pick |= (place // 16 == peer) & (line // 4 == z) & (place % 4 == line % 4)
    pick = pick.astype(f32).astype(bf16)
    pick_ref[...] = pick
    rank = iota((16, 256), 0) + 16 * lax.axis_index("fsdp")
    rank = 32 * (rank // 4 % 2) + 4 * (rank // 8) + rank % 4
    for i in range(3):
        put_ref[16 * i : 16 * i + 16, :] = (iota((16, 256), 1) == rank + 64 * i).astype(f32).astype(bf16)
    copies[0].wait()
    tokens = jnp.concatenate([hidden_ref[0].astype(f32), hidden_ref[1].astype(f32)], axis=0)
    copies[1].wait()
    terms = [t.astype(f32) for t in split3(dot(tokens.astype(bf16), frozen_ref[...], NN))]
    terms_ref[...] = jnp.concatenate(terms + [jnp.zeros((4, 256), f32)], axis=0)


def pack_queries(own_ref, other_ref, terms_ref, pick_ref, put_ref, factors_ref, out_ref, columns, spread):
    ylo = lax.axis_index("ylo")
    low_half = iota((16, 128), 1) < 64
    here = iota((16, 256), 1) // 64 == iota((16, 256), 0) // 4
    for z in range(8):
        columns[:, 384 * z : 384 * z + 384] = factors_ref[z]
        last = factors_ref[z, :, 256:384].astype(f32)
        rows = jnp.where(low_half, pltpu.roll(last, 64, 1), last)
        rows = jnp.where(here, jnp.concatenate([rows, rows], axis=1), 0.0)
        spread[16 * z : 16 * z + 16, :] = rows.astype(bf16)
    tokens = jnp.concatenate([own_ref[...].astype(f32), other_ref[...].astype(f32)], axis=0).astype(bf16)
    low = dot(tokens, columns[...], NT)
    up = dot(pick_ref[...], spread[...], NN).astype(bf16)
    lanes = jnp.zeros((8, 256), f32)
    for i, term in enumerate(split3(low)):
        lanes += dot(term, put_ref[16 * i : 16 * i + 16, :], NN)
    tails = []
    for y in range(2):
        part = jnp.where(ylo == y, lanes[0:4], lanes[4:8])
        tails.append(jnp.concatenate([terms_ref[0:12, :], part], axis=0).astype(bf16))
    for peer, y in enumerate(y_order):
        out_ref[peer, 0:32, :] = up
        out_ref[peer, 32:48, :] = tails[y % 2]


def attend(parts_ref, gain_ref, keys_ref, values_ref, new_keys_ref, new_values_ref, lengths_ref, out_ref, queries, fresh_k, fresh_v):
    f = lax.axis_index("fsdp")
    upper = lax.axis_index("ylo") == 1
    peers = [y_order.index(y) for y in range(8)]
    tails = [parts_ref[i, 32:48, :].astype(f32) for i in peers]
    low = [tails[y][12:16] + tails[2 + y][12:16] + tails[4 + y][12:16] + tails[6 + y][12:16] for y in range(2)]
    low = jnp.concatenate(low, axis=0)
    low = jnp.concatenate([low[:, :128], low[:, 128:]], axis=0).astype(bf16)
    for i in range(4):
        up = jnp.concatenate([parts_ref[peers[2 * i], 0:32, :], parts_ref[peers[2 * i + 1], 0:32, :]] * 2, axis=0)
        tail = jnp.where(upper, tails[2 * i + 1], tails[2 * i])
        adapter = dot(low, up, NN)
        adapter = adapter[0:8] + adapter[8:16]
        adapter = adapter[0:4] + adapter[4:8]
        query = tail[0:4] + tail[4:8] + tail[8:12] + adapter_scale * adapter
        for j in range(2):
            at = 8 * i + 4 * j
            queries[at : at + 4, :] = query[:, 128 * j : 128 * j + 128]
    query = queries[...]
    mean = jnp.mean(query * query, axis=-1, keepdims=True)
    normed = (query * lax.rsqrt(mean + norm_epsilon) * gain_ref[...]).astype(bf16)
    span = keys_ref.shape[1]
    fresh_k[...] = jnp.zeros_like(fresh_k)
    fresh_v[...] = jnp.zeros_like(fresh_v)
    for i in range(2):
        fresh_k[2 * i : 2 * i + 2, :] = new_keys_ref[i].astype(f32)
        fresh_v[2 * i : 2 * i + 2, :] = new_values_ref[i].astype(f32)
    scale = 128 ** (-0.5)
    first = iota((32, 128), 0) % 4 < 2
    nothing = jnp.zeros_like(normed)
    both = jnp.concatenate([jnp.where(first, normed, nothing), jnp.where(first, nothing, normed)], axis=1)
    scores = dot(both, jnp.concatenate([keys_ref[0], keys_ref[1]], axis=1), NT) * scale
    lengths = lengths_ref[...]
    limit = jnp.where(iota((32, 1), 0) % 4 < 2, lengths[:, 0:1], lengths[:, 1:2]) - f * span
    scores = jnp.where(iota((32, span), 1) < limit, scores, masked_score)
    line, place = iota((32, 16), 0), iota((32, 16), 1)
    fresh = dot(normed, fresh_k[...].astype(bf16), NT) * scale
    fresh_valid = (place // 2 == (line % 4) // 2) & (place % 2 <= line % 2) & (f == 0)
    fresh = jnp.where(fresh_valid, fresh, masked_score)
    top = jnp.maximum(jnp.max(scores, axis=-1, keepdims=True), jnp.max(fresh, axis=-1, keepdims=True))
    weights = jnp.exp(scores - top)
    fresh_weights = jnp.exp(fresh - top)
    total = jnp.sum(weights, axis=-1, keepdims=True) + jnp.sum(fresh_weights, axis=-1, keepdims=True)
    mixed = dot(weights.astype(bf16), jnp.concatenate([values_ref[0], values_ref[1]], axis=1), NN)
    mixed = jnp.where(first, mixed[:, :128], mixed[:, 128:])
    mixed += dot(fresh_weights.astype(bf16), fresh_v[...].astype(bf16), NN)
    tops, totals = jnp.broadcast_to(top, (32, 128)), jnp.broadcast_to(total, (32, 128))
    for peer, i in enumerate(fsdp_order):
        out_ref[peer, 0:8, :] = mixed[8 * i : 8 * i + 8]
        out_ref[peer, 8:16, :] = tops[8 * i : 8 * i + 8]
        out_ref[peer, 16:24, :] = totals[8 * i : 8 * i + 8]


def merge(parts_ref, out_ref):
    tops = [parts_ref[i, 8:16, :] for i in range(4)]
    top = jnp.maximum(jnp.maximum(tops[0], tops[1]), jnp.maximum(tops[2], tops[3]))
    total = jnp.zeros((8, 128), f32)
    mixed = jnp.zeros((8, 128), f32)
    for i in range(4):
        scale = jnp.exp(tops[i] - top)
        total += scale * parts_ref[i, 16:24, :]
        mixed += scale * parts_ref[i, 0:8, :]
    result = mixed / total
    for i in range(2):
        for j in range(2):
            out_ref[i, :, 128 * j : 128 * j + 128] = result[4 * j + 2 * i : 4 * j + 2 * i + 2].astype(bf16)


room = pltpu.CompilerParams(vmem_limit_bytes=8 * 2**20)


def exchange(x, axis, order):
    return lax.all_to_all(x, axis, 0, 0, axis_index_groups=[list(order)])


def whole(n):
    return [pl.BlockSpec(memory_space=pltpu.VMEM)] * n


def hbm(n):
    return [pl.BlockSpec(memory_space=pltpu.HBM)] * n


def far(x):
    return pltpu.with_memory_space_constraint(x, pltpu.HBM)


def on_device(
    hidden_in,
    frozen_query_matrix,
    factor_down,
    factor_up,
    query_gain,
    key_cache,
    value_cache,
    new_keys,
    new_values,
    cache_lengths,
):
    packed, own, lent = pl.pallas_call(
        pack_factors,
        out_shape=(
            jax.ShapeDtypeStruct((8, 16, 384), bf16),
            pltpu.VMEM((4, 8 * 384), bf16),
            jax.ShapeDtypeStruct((4, 8 * 384), bf16),
        ),
        in_specs=hbm(3),
        out_specs=(hbm(1)[0], *whole(2)),
        scratch_shapes=[
            pltpu.VMEM((64, 320), bf16),
            pltpu.VMEM((4, 256), bf16),
            pltpu.VMEM((2, 2, 5120), bf16),
            pltpu.VMEM((16, 128), f32),
            pltpu.VMEM((16, 384), bf16),
            pltpu.VMEM((4, 5120), f32),
            pltpu.SemaphoreType.DMA((11,)),
        ],
        compiler_params=room,
        name="pack_factors",
    )(far(factor_down.T), far(factor_up), far(hidden_in))
    factors = exchange(packed, "z", z_order)
    other = lax.ppermute(lent, "ylo", ((0, 1), (1, 0)))
    terms, pick, put = pl.pallas_call(
        project,
        out_shape=(
            jax.ShapeDtypeStruct((16, 256), f32),
            jax.ShapeDtypeStruct((32, 128), bf16),
            jax.ShapeDtypeStruct((48, 256), bf16),
        ),
        in_specs=hbm(2),
        out_specs=tuple(whole(3)),
        scratch_shapes=[
            pltpu.VMEM((2, 2, 5120), bf16),
            pltpu.VMEM((5120, 256), bf16),
            pltpu.SemaphoreType.DMA((2,)),
        ],
        compiler_params=room,
        cost_estimate=pl.CostEstimate(flops=2 * 4 * 5120 * 256, bytes_accessed=8 * 2**20, transcendentals=0),
        name="project",
    )(far(hidden_in), far(frozen_query_matrix))
    sent = pl.pallas_call(
        pack_queries,
        out_shape=jax.ShapeDtypeStruct((8, 48, 256), bf16),
        in_specs=whole(6),
        out_specs=whole(1)[0],
        scratch_shapes=[pltpu.VMEM((16, 8 * 384), bf16), pltpu.VMEM((128, 256), bf16)],
        compiler_params=room,
        name="pack_queries",
    )(own, other, terms, pick, put, factors)
    parts = exchange(sent, ("fsdp", "ylo"), y_order)
    partial = pl.pallas_call(
        attend,
        out_shape=jax.ShapeDtypeStruct((4, 24, 128), f32),
        in_specs=whole(7),
        out_specs=whole(1)[0],
        scratch_shapes=[pltpu.VMEM((32, 128), f32)] + [pltpu.VMEM((16, 128), f32)] * 2,
        compiler_params=room,
        name="attend",
    )(parts, query_gain.reshape(1, 128), key_cache, value_cache, new_keys, new_values, cache_lengths.reshape(1, 2))
    partial = exchange(partial, "fsdp", fsdp_order)
    return pl.pallas_call(
        merge,
        out_shape=jax.ShapeDtypeStruct((2, 2, 256), bf16),
        in_specs=whole(1),
        out_specs=whole(1)[0],
        compiler_params=room,
        name="merge",
    )(partial)


def solution(mesh):
    rep = ("z", "ylo")
    lines = mesh.devices.reshape(mesh.devices.shape[0] // 2, 2, *mesh.devices.shape[1:])
    lines = jax.sharding.Mesh(lines, rep + mesh.axis_names[1:])
    placed = (
        P(rep, None, None),
        P(None, ("tp", "fsdp")),
        P(rep, None),
        P(rep, ("tp", "fsdp")),
        P(),
        P(rep, "fsdp", "tp"),
        P(rep, "fsdp", "tp"),
        P(rep, None, "tp"),
        P(rep, None, "tp"),
        P(rep),
    )
    return jax.shard_map(
        on_device,
        mesh=lines,
        in_specs=placed,
        out_specs=P(rep, None, ("tp", "fsdp")),
        check_vma=False,
    )
```

```python
import jax
import jax.numpy as jnp
from jax import lax
from jax.experimental import pallas as pl
from jax.experimental.pallas import tpu as pltpu
from jax.sharding import PartitionSpec as P

adapter_scale = 2.0
norm_epsilon = 1e-06
masked_score = -1e30

z_order = (6, 7, 0, 1, 2, 3, 4, 5)
y_order = (5, 1, 0, 2, 3, 4, 6, 7)
fsdp_order = (2, 3, 0, 1)

NT = (((1,), (1,)), ((), ()))
NN = (((1,), (0,)), ((), ()))
f32, bf16 = jnp.float32, jnp.bfloat16


def dot(a, b, dims):
    return lax.dot_general(a, b, dims, preferred_element_type=f32)


def iota(shape, axis):
    return lax.broadcasted_iota(jnp.int32, shape, axis)


def split3(x):
    hi = x.astype(bf16)
    rest = x - hi.astype(f32)
    mid = rest.astype(bf16)
    lo = (rest - mid.astype(f32)).astype(bf16)
    return hi, mid, lo


def pack_factors(down_hbm, up_hbm, hidden_hbm, out_hbm, own_ref, other_ref, down_ref, up_ref, hidden_ref, rows_ref, packed, tokens, sems):
    down_copy = pltpu.make_async_copy(down_hbm, down_ref, sems.at[0])
    up_copy = pltpu.make_async_copy(up_hbm, up_ref, sems.at[1])
    hidden_copy = pltpu.make_async_copy(hidden_hbm, hidden_ref, sems.at[2])
    down_copy.start()
    up_copy.start()
    hidden_copy.start()
    up_copy.wait()
    up = up_ref[...].astype(f32)
    for i in range(2):
        half = up[:, 128 * i : 128 * i + 128]
        rows_ref[8 * i : 8 * i + 4, :] = pltpu.roll(half, 64, 1)
        rows_ref[8 * i + 4 : 8 * i + 8, :] = half
    down_copy.wait()
    start = pl.multiple_of(16 * lax.axis_index("fsdp"), 16)
    columns = down_ref[pl.ds(start, 16), :].astype(f32)
    last = jnp.concatenate([columns[:, 256:], jnp.zeros((16, 64), f32)], axis=1)
    last = jnp.where(iota((16, 128), 1) < 64, last, rows_ref[...])
    packed[...] = jnp.concatenate([columns[:, :256], last], axis=1).astype(bf16)
    out_copies = [pltpu.make_async_copy(packed, out_hbm.at[peer], sems.at[3 + peer]) for peer in range(8)]
    for copy in out_copies:
        copy.start()
    hidden_copy.wait()
    upper = lax.axis_index("ylo") == 1
    for i in range(2):
        tokens[2 * i : 2 * i + 2, :] = hidden_ref[i].astype(f32)
    low = iota((4, 128), 1) < 64
    for peer, z in enumerate(z_order):
        tiles = [tokens[:, 640 * z + 128 * i : 640 * z + 128 * i + 128] for i in range(5)]
        turned = [pltpu.roll(tile, 64, 1) for tile in tiles[2:]] + [jnp.zeros((4, 128), f32)]
        for i in range(3):
            shifted = jnp.where(low, turned[i], turned[i + 1])
            plain = tiles[i] if i < 2 else jnp.where(low, tiles[2], 0.0)
            at = 384 * peer + 128 * i
            own_ref[:, at : at + 128] = jnp.where(upper, shifted, plain).astype(bf16)
            other_ref[:, at : at + 128] = jnp.where(upper, plain, shifted).astype(bf16)
    for copy in out_copies:
        copy.wait()


def project(hidden_hbm, frozen_hbm, keys_hbm, values_hbm, terms_ref, pick_ref, put_ref, keys_ref, values_ref, hidden_ref, frozen_ref, sems):
    copies = [
        pltpu.make_async_copy(source, target, sems.at[i])
        for i, (source, target) in enumerate(
            (
                (hidden_hbm, hidden_ref),
                (frozen_hbm, frozen_ref),
                (keys_hbm, keys_ref),
                (values_hbm, values_ref),
            )
        )
    ]
    for copy in copies:
        copy.start()
    line, place = iota((32, 128), 0), iota((32, 128), 1)
    pick = jnp.zeros((32, 128), jnp.bool_)
    for peer, z in enumerate(z_order):
        pick |= (place // 16 == peer) & (line // 4 == z) & (place % 4 == line % 4)
    pick = pick.astype(f32).astype(bf16)
    pick_ref[...] = pick
    rank = iota((16, 256), 0) + 16 * lax.axis_index("fsdp")
    rank = 32 * (rank // 4 % 2) + 4 * (rank // 8) + rank % 4
    for i in range(3):
        put_ref[16 * i : 16 * i + 16, :] = (iota((16, 256), 1) == rank + 64 * i).astype(f32).astype(bf16)
    copies[0].wait()
    tokens = jnp.concatenate([hidden_ref[0].astype(f32), hidden_ref[1].astype(f32)], axis=0)
    copies[1].wait()
    terms = [t.astype(f32) for t in split3(dot(tokens.astype(bf16), frozen_ref[...], NN))]
    terms_ref[...] = jnp.concatenate(terms + [jnp.zeros((4, 256), f32)], axis=0)
    copies[2].wait()
    copies[3].wait()


def pack_queries(own_ref, other_ref, terms_ref, pick_ref, put_ref, factors_ref, out_ref, columns, spread):
    ylo = lax.axis_index("ylo")
    low_half = iota((16, 128), 1) < 64
    here = iota((16, 256), 1) // 64 == iota((16, 256), 0) // 4
    for z in range(8):
        columns[:, 384 * z : 384 * z + 384] = factors_ref[z]
        last = factors_ref[z, :, 256:384].astype(f32)
        rows = jnp.where(low_half, pltpu.roll(last, 64, 1), last)
        rows = jnp.where(here, jnp.concatenate([rows, rows], axis=1), 0.0)
        spread[16 * z : 16 * z + 16, :] = rows.astype(bf16)
    tokens = jnp.concatenate([own_ref[...].astype(f32), other_ref[...].astype(f32)], axis=0).astype(bf16)
    low = dot(tokens, columns[...], NT)
    up = dot(pick_ref[...], spread[...], NN).astype(bf16)
    lanes = jnp.zeros((8, 256), f32)
    for i, term in enumerate(split3(low)):
        lanes += dot(term, put_ref[16 * i : 16 * i + 16, :], NN)
    tails = []
    for y in range(2):
        part = jnp.where(ylo == y, lanes[0:4], lanes[4:8])
        tails.append(jnp.concatenate([terms_ref[0:12, :], part], axis=0).astype(bf16))
    for peer, y in enumerate(y_order):
        out_ref[peer, 0:32, :] = up
        out_ref[peer, 32:48, :] = tails[y % 2]


def attend(parts_ref, gain_ref, keys_ref, values_ref, new_keys_ref, new_values_ref, lengths_ref, out_ref, queries, fresh_k, fresh_v):
    f = lax.axis_index("fsdp")
    upper = lax.axis_index("ylo") == 1
    peers = [y_order.index(y) for y in range(8)]
    tails = [parts_ref[i, 32:48, :].astype(f32) for i in peers]
    low = [tails[y][12:16] + tails[2 + y][12:16] + tails[4 + y][12:16] + tails[6 + y][12:16] for y in range(2)]
    low = jnp.concatenate(low, axis=0)
    low = jnp.concatenate([low[:, :128], low[:, 128:]], axis=0).astype(bf16)
    for i in range(4):
        up = jnp.concatenate([parts_ref[peers[2 * i], 0:32, :], parts_ref[peers[2 * i + 1], 0:32, :]] * 2, axis=0)
        tail = jnp.where(upper, tails[2 * i + 1], tails[2 * i])
        adapter = dot(low, up, NN)
        adapter = adapter[0:8] + adapter[8:16]
        adapter = adapter[0:4] + adapter[4:8]
        query = tail[0:4] + tail[4:8] + tail[8:12] + adapter_scale * adapter
        for j in range(2):
            at = 8 * i + 4 * j
            queries[at : at + 4, :] = query[:, 128 * j : 128 * j + 128]
    query = queries[...]
    mean = jnp.mean(query * query, axis=-1, keepdims=True)
    normed = (query * lax.rsqrt(mean + norm_epsilon) * gain_ref[...]).astype(bf16)
    span = keys_ref.shape[1]
    fresh_k[...] = jnp.zeros_like(fresh_k)
    fresh_v[...] = jnp.zeros_like(fresh_v)
    for i in range(2):
        fresh_k[2 * i : 2 * i + 2, :] = new_keys_ref[i].astype(f32)
        fresh_v[2 * i : 2 * i + 2, :] = new_values_ref[i].astype(f32)
    scale = 128 ** (-0.5)
    first = iota((32, 128), 0) % 4 < 2
    nothing = jnp.zeros_like(normed)
    both = jnp.concatenate([jnp.where(first, normed, nothing), jnp.where(first, nothing, normed)], axis=1)
    scores = dot(both, jnp.concatenate([keys_ref[0], keys_ref[1]], axis=1), NT) * scale
    lengths = lengths_ref[...]
    limit = jnp.where(iota((32, 1), 0) % 4 < 2, lengths[:, 0:1], lengths[:, 1:2]) - f * span
    scores = jnp.where(iota((32, span), 1) < limit, scores, masked_score)
    line, place = iota((32, 16), 0), iota((32, 16), 1)
    fresh = dot(normed, fresh_k[...].astype(bf16), NT) * scale
    fresh_valid = (place // 2 == (line % 4) // 2) & (place % 2 <= line % 2) & (f == 0)
    fresh = jnp.where(fresh_valid, fresh, masked_score)
    top = jnp.maximum(jnp.max(scores, axis=-1, keepdims=True), jnp.max(fresh, axis=-1, keepdims=True))
    weights = jnp.exp(scores - top)
    fresh_weights = jnp.exp(fresh - top)
    total = jnp.sum(weights, axis=-1, keepdims=True) + jnp.sum(fresh_weights, axis=-1, keepdims=True)
    mixed = dot(weights.astype(bf16), jnp.concatenate([values_ref[0], values_ref[1]], axis=1), NN)
    mixed = jnp.where(first, mixed[:, :128], mixed[:, 128:])
    mixed += dot(fresh_weights.astype(bf16), fresh_v[...].astype(bf16), NN)
    tops, totals = jnp.broadcast_to(top, (32, 128)), jnp.broadcast_to(total, (32, 128))
    for peer, i in enumerate(fsdp_order):
        out_ref[peer, 0:8, :] = mixed[8 * i : 8 * i + 8]
        out_ref[peer, 8:16, :] = tops[8 * i : 8 * i + 8]
        out_ref[peer, 16:24, :] = totals[8 * i : 8 * i + 8]


def merge(parts_ref, out_ref):
    tops = [parts_ref[i, 8:16, :] for i in range(4)]
    top = jnp.maximum(jnp.maximum(tops[0], tops[1]), jnp.maximum(tops[2], tops[3]))
    total = jnp.zeros((8, 128), f32)
    mixed = jnp.zeros((8, 128), f32)
    for i in range(4):
        scale = jnp.exp(tops[i] - top)
        total += scale * parts_ref[i, 16:24, :]
        mixed += scale * parts_ref[i, 0:8, :]
    result = mixed / total
    for i in range(2):
        for j in range(2):
            out_ref[i, :, 128 * j : 128 * j + 128] = result[4 * j + 2 * i : 4 * j + 2 * i + 2].astype(bf16)


room = pltpu.CompilerParams(vmem_limit_bytes=8 * 2**20)


def exchange(x, axis, order):
    return lax.all_to_all(x, axis, 0, 0, axis_index_groups=[list(order)])


def whole(n):
    return [pl.BlockSpec(memory_space=pltpu.VMEM)] * n


def hbm(n):
    return [pl.BlockSpec(memory_space=pltpu.HBM)] * n


def far(x):
    return pltpu.with_memory_space_constraint(x, pltpu.HBM)


def on_device(
    hidden_in,
    frozen_query_matrix,
    factor_down,
    factor_up,
    query_gain,
    key_cache,
    value_cache,
    new_keys,
    new_values,
    cache_lengths,
):
    packed, own, lent = pl.pallas_call(
        pack_factors,
        out_shape=(
            jax.ShapeDtypeStruct((8, 16, 384), bf16),
            pltpu.VMEM((4, 8 * 384), bf16),
            jax.ShapeDtypeStruct((4, 8 * 384), bf16),
        ),
        in_specs=hbm(3),
        out_specs=(hbm(1)[0], *whole(2)),
        scratch_shapes=[
            pltpu.VMEM((64, 320), bf16),
            pltpu.VMEM((4, 256), bf16),
            pltpu.VMEM((2, 2, 5120), bf16),
            pltpu.VMEM((16, 128), f32),
            pltpu.VMEM((16, 384), bf16),
            pltpu.VMEM((4, 5120), f32),
            pltpu.SemaphoreType.DMA((11,)),
        ],
        compiler_params=room,
        name="pack_factors",
    )(far(factor_down.T), far(factor_up), far(hidden_in))
    factors = exchange(packed, "z", z_order)
    other = lax.ppermute(lent, "ylo", ((0, 1), (1, 0)))
    terms, pick, put, keys, values = pl.pallas_call(
        project,
        out_shape=(
            jax.ShapeDtypeStruct((16, 256), f32),
            jax.ShapeDtypeStruct((32, 128), bf16),
            jax.ShapeDtypeStruct((48, 256), bf16),
            pltpu.VMEM(key_cache.shape, bf16),
            pltpu.VMEM(value_cache.shape, bf16),
        ),
        in_specs=hbm(4),
        out_specs=tuple(whole(5)),
        scratch_shapes=[
            pltpu.VMEM((2, 2, 5120), bf16),
            pltpu.VMEM((5120, 256), bf16),
            pltpu.SemaphoreType.DMA((4,)),
        ],
        compiler_params=room,
        cost_estimate=pl.CostEstimate(flops=2 * 4 * 5120 * 256, bytes_accessed=8 * 2**20, transcendentals=0),
        name="project",
    )(far(hidden_in), far(frozen_query_matrix), far(key_cache), far(value_cache))
    sent = pl.pallas_call(
        pack_queries,
        out_shape=jax.ShapeDtypeStruct((8, 48, 256), bf16),
        in_specs=whole(6),
        out_specs=whole(1)[0],
        scratch_shapes=[pltpu.VMEM((16, 8 * 384), bf16), pltpu.VMEM((128, 256), bf16)],
        compiler_params=room,
        name="pack_queries",
    )(own, other, terms, pick, put, factors)
    parts = exchange(sent, ("fsdp", "ylo"), y_order)
    partial = pl.pallas_call(
        attend,
        out_shape=jax.ShapeDtypeStruct((4, 24, 128), f32),
        in_specs=whole(7),
        out_specs=whole(1)[0],
        scratch_shapes=[pltpu.VMEM((32, 128), f32)] + [pltpu.VMEM((16, 128), f32)] * 2,
        compiler_params=room,
        name="attend",
    )(parts, query_gain.reshape(1, 128), keys, values, new_keys, new_values, cache_lengths.reshape(1, 2))
    partial = exchange(partial, "fsdp", fsdp_order)
    return pl.pallas_call(
        merge,
        out_shape=jax.ShapeDtypeStruct((2, 2, 256), bf16),
        in_specs=whole(1),
        out_specs=whole(1)[0],
        compiler_params=room,
        name="merge",
    )(partial)


def solution(mesh):
    rep = ("z", "ylo")
    lines = mesh.devices.reshape(mesh.devices.shape[0] // 2, 2, *mesh.devices.shape[1:])
    lines = jax.sharding.Mesh(lines, rep + mesh.axis_names[1:])
    placed = (
        P(rep, None, None),
        P(None, ("tp", "fsdp")),
        P(rep, None),
        P(rep, ("tp", "fsdp")),
        P(),
        P(rep, "fsdp", "tp"),
        P(rep, "fsdp", "tp"),
        P(rep, None, "tp"),
        P(rep, None, "tp"),
        P(rep),
    )
    return jax.shard_map(
        on_device,
        mesh=lines,
        in_specs=placed,
        out_specs=P(rep, None, ("tp", "fsdp")),
        check_vma=False,
    )
```

```python
import jax
import jax.numpy as jnp
from jax import lax
from jax.experimental import pallas as pl
from jax.experimental.pallas import tpu as pltpu
from jax.sharding import PartitionSpec as P

adapter_scale = 2.0
norm_epsilon = 1e-06
masked_score = -1e30

z_order = (6, 7, 5, 0, 4, 1, 3, 2)
y_order = (5, 1, 0, 2, 3, 4, 6, 7)
fsdp_order = (2, 3, 0, 1)

NT = (((1,), (1,)), ((), ()))
NN = (((1,), (0,)), ((), ()))
f32, bf16 = jnp.float32, jnp.bfloat16


def dot(a, b, dims):
    return lax.dot_general(a, b, dims, preferred_element_type=f32)


def iota(shape, axis):
    return lax.broadcasted_iota(jnp.int32, shape, axis)


def split3(x):
    hi = x.astype(bf16)
    rest = x - hi.astype(f32)
    mid = rest.astype(bf16)
    lo = (rest - mid.astype(f32)).astype(bf16)
    return hi, mid, lo


def pack_factors(down_hbm, up_hbm, hidden_hbm, out_hbm, own_ref, other_ref, down_ref, up_ref, hidden_ref, rows_ref, packed, tokens, sems):
    down_copy = pltpu.make_async_copy(down_hbm, down_ref, sems.at[0])
    up_copy = pltpu.make_async_copy(up_hbm, up_ref, sems.at[1])
    hidden_copy = pltpu.make_async_copy(hidden_hbm, hidden_ref, sems.at[2])
    down_copy.start()
    up_copy.start()
    hidden_copy.start()
    up_copy.wait()
    up = up_ref[...].astype(f32)
    for i in range(2):
        half = up[:, 128 * i : 128 * i + 128]
        rows_ref[8 * i : 8 * i + 4, :] = pltpu.roll(half, 64, 1)
        rows_ref[8 * i + 4 : 8 * i + 8, :] = half
    down_copy.wait()
    start = pl.multiple_of(16 * lax.axis_index("fsdp"), 16)
    columns = down_ref[pl.ds(start, 16), :].astype(f32)
    last = jnp.concatenate([columns[:, 256:], jnp.zeros((16, 64), f32)], axis=1)
    last = jnp.where(iota((16, 128), 1) < 64, last, rows_ref[...])
    packed[...] = jnp.concatenate([columns[:, :256], last], axis=1).astype(bf16)
    out_copies = [pltpu.make_async_copy(packed, out_hbm.at[peer], sems.at[3 + peer]) for peer in range(8)]
    for copy in out_copies:
        copy.start()
    hidden_copy.wait()
    upper = lax.axis_index("ylo") == 1
    for i in range(2):
        tokens[2 * i : 2 * i + 2, :] = hidden_ref[i].astype(f32)
    low = iota((4, 128), 1) < 64
    for peer, z in enumerate(z_order):
        tiles = [tokens[:, 640 * z + 128 * i : 640 * z + 128 * i + 128] for i in range(5)]
        turned = [pltpu.roll(tile, 64, 1) for tile in tiles[2:]] + [jnp.zeros((4, 128), f32)]
        for i in range(3):
            shifted = jnp.where(low, turned[i], turned[i + 1])
            plain = tiles[i] if i < 2 else jnp.where(low, tiles[2], 0.0)
            at = 384 * peer + 128 * i
            own_ref[:, at : at + 128] = jnp.where(upper, shifted, plain).astype(bf16)
            other_ref[:, at : at + 128] = jnp.where(upper, plain, shifted).astype(bf16)
    for copy in out_copies:
        copy.wait()


def project(hidden_hbm, frozen_hbm, keys_hbm, values_hbm, terms_ref, pick_ref, put_ref, keys_ref, values_ref, hidden_ref, frozen_ref, sems):
    copies = [
        pltpu.make_async_copy(source, target, sems.at[i])
        for i, (source, target) in enumerate(
            (
                (hidden_hbm, hidden_ref),
                (frozen_hbm, frozen_ref),
                (keys_hbm, keys_ref),
                (values_hbm, values_ref),
            )
        )
    ]
    for copy in copies:
        copy.start()
    line, place = iota((32, 128), 0), iota((32, 128), 1)
    pick = jnp.zeros((32, 128), jnp.bool_)
    for peer, z in enumerate(z_order):
        pick |= (place // 16 == peer) & (line // 4 == z) & (place % 4 == line % 4)
    pick = pick.astype(f32).astype(bf16)
    pick_ref[...] = pick
    rank = iota((16, 256), 0) + 16 * lax.axis_index("fsdp")
    rank = 32 * (rank // 4 % 2) + 4 * (rank // 8) + rank % 4
    for i in range(3):
        put_ref[16 * i : 16 * i + 16, :] = (iota((16, 256), 1) == rank + 64 * i).astype(f32).astype(bf16)
    copies[0].wait()
    tokens = jnp.concatenate([hidden_ref[0].astype(f32), hidden_ref[1].astype(f32)], axis=0)
    copies[1].wait()
    terms = [t.astype(f32) for t in split3(dot(tokens.astype(bf16), frozen_ref[...], NN))]
    terms_ref[...] = jnp.concatenate(terms + [jnp.zeros((4, 256), f32)], axis=0)
    copies[2].wait()
    copies[3].wait()


def pack_queries(own_ref, other_ref, terms_ref, pick_ref, put_ref, factors_ref, out_ref, columns, spread):
    ylo = lax.axis_index("ylo")
    low_half = iota((16, 128), 1) < 64
    here = iota((16, 256), 1) // 64 == iota((16, 256), 0) // 4
    for z in range(8):
        columns[:, 384 * z : 384 * z + 384] = factors_ref[z]
        last = factors_ref[z, :, 256:384].astype(f32)
        rows = jnp.where(low_half, pltpu.roll(last, 64, 1), last)
        rows = jnp.where(here, jnp.concatenate([rows, rows], axis=1), 0.0)
        spread[16 * z : 16 * z + 16, :] = rows.astype(bf16)
    tokens = jnp.concatenate([own_ref[...].astype(f32), other_ref[...].astype(f32)], axis=0).astype(bf16)
    low = dot(tokens, columns[...], NT)
    up = dot(pick_ref[...], spread[...], NN).astype(bf16)
    lanes = jnp.zeros((8, 256), f32)
    for i, term in enumerate(split3(low)):
        lanes += dot(term, put_ref[16 * i : 16 * i + 16, :], NN)
    tails = []
    for y in range(2):
        part = jnp.where(ylo == y, lanes[0:4], lanes[4:8])
        tails.append(jnp.concatenate([terms_ref[0:12, :], part], axis=0).astype(bf16))
    for peer, y in enumerate(y_order):
        out_ref[peer, 0:32, :] = up
        out_ref[peer, 32:48, :] = tails[y % 2]


def attend(parts_ref, gain_ref, keys_ref, values_ref, new_keys_ref, new_values_ref, lengths_ref, out_ref, queries, fresh_k, fresh_v):
    f = lax.axis_index("fsdp")
    upper = lax.axis_index("ylo") == 1
    peers = [y_order.index(y) for y in range(8)]
    tails = [parts_ref[i, 32:48, :].astype(f32) for i in peers]
    low = [tails[y][12:16] + tails[2 + y][12:16] + tails[4 + y][12:16] + tails[6 + y][12:16] for y in range(2)]
    low = jnp.concatenate(low, axis=0)
    low = jnp.concatenate([low[:, :128], low[:, 128:]], axis=0).astype(bf16)
    for i in range(4):
        up = jnp.concatenate([parts_ref[peers[2 * i], 0:32, :], parts_ref[peers[2 * i + 1], 0:32, :]] * 2, axis=0)
        tail = jnp.where(upper, tails[2 * i + 1], tails[2 * i])
        adapter = dot(low, up, NN)
        adapter = adapter[0:8] + adapter[8:16]
        adapter = adapter[0:4] + adapter[4:8]
        query = tail[0:4] + tail[4:8] + tail[8:12] + adapter_scale * adapter
        for j in range(2):
            at = 8 * i + 4 * j
            queries[at : at + 4, :] = query[:, 128 * j : 128 * j + 128]
    query = queries[...]
    mean = jnp.mean(query * query, axis=-1, keepdims=True)
    normed = (query * lax.rsqrt(mean + norm_epsilon) * gain_ref[...]).astype(bf16)
    span = keys_ref.shape[1]
    fresh_k[...] = jnp.zeros_like(fresh_k)
    fresh_v[...] = jnp.zeros_like(fresh_v)
    for i in range(2):
        fresh_k[2 * i : 2 * i + 2, :] = new_keys_ref[i].astype(f32)
        fresh_v[2 * i : 2 * i + 2, :] = new_values_ref[i].astype(f32)
    scale = 128 ** (-0.5)
    first = iota((32, 128), 0) % 4 < 2
    nothing = jnp.zeros_like(normed)
    both = jnp.concatenate([jnp.where(first, normed, nothing), jnp.where(first, nothing, normed)], axis=1)
    scores = dot(both, jnp.concatenate([keys_ref[0], keys_ref[1]], axis=1), NT) * scale
    lengths = lengths_ref[...]
    limit = jnp.where(iota((32, 1), 0) % 4 < 2, lengths[:, 0:1], lengths[:, 1:2]) - f * span
    scores = jnp.where(iota((32, span), 1) < limit, scores, masked_score)
    line, place = iota((32, 16), 0), iota((32, 16), 1)
    fresh = dot(normed, fresh_k[...].astype(bf16), NT) * scale
    fresh_valid = (place // 2 == (line % 4) // 2) & (place % 2 <= line % 2) & (f == 0)
    fresh = jnp.where(fresh_valid, fresh, masked_score)
    top = jnp.maximum(jnp.max(scores, axis=-1, keepdims=True), jnp.max(fresh, axis=-1, keepdims=True))
    weights = jnp.exp(scores - top)
    fresh_weights = jnp.exp(fresh - top)
    total = jnp.sum(weights, axis=-1, keepdims=True) + jnp.sum(fresh_weights, axis=-1, keepdims=True)
    mixed = dot(weights.astype(bf16), jnp.concatenate([values_ref[0], values_ref[1]], axis=1), NN)
    mixed = jnp.where(first, mixed[:, :128], mixed[:, 128:])
    mixed += dot(fresh_weights.astype(bf16), fresh_v[...].astype(bf16), NN)
    tops, totals = jnp.broadcast_to(top, (32, 128)), jnp.broadcast_to(total, (32, 128))
    for peer, i in enumerate(fsdp_order):
        out_ref[peer, 0:8, :] = mixed[8 * i : 8 * i + 8]
        out_ref[peer, 8:16, :] = tops[8 * i : 8 * i + 8]
        out_ref[peer, 16:24, :] = totals[8 * i : 8 * i + 8]


def merge(parts_ref, out_ref):
    tops = [parts_ref[i, 8:16, :] for i in range(4)]
    top = jnp.maximum(jnp.maximum(tops[0], tops[1]), jnp.maximum(tops[2], tops[3]))
    total = jnp.zeros((8, 128), f32)
    mixed = jnp.zeros((8, 128), f32)
    for i in range(4):
        scale = jnp.exp(tops[i] - top)
        total += scale * parts_ref[i, 16:24, :]
        mixed += scale * parts_ref[i, 0:8, :]
    result = mixed / total
    for i in range(2):
        for j in range(2):
            out_ref[i, :, 128 * j : 128 * j + 128] = result[4 * j + 2 * i : 4 * j + 2 * i + 2].astype(bf16)


room = pltpu.CompilerParams(vmem_limit_bytes=8 * 2**20)


def exchange(x, axis, order):
    return lax.all_to_all(x, axis, 0, 0, axis_index_groups=[list(order)])


def whole(n):
    return [pl.BlockSpec(memory_space=pltpu.VMEM)] * n


def hbm(n):
    return [pl.BlockSpec(memory_space=pltpu.HBM)] * n


def far(x):
    return pltpu.with_memory_space_constraint(x, pltpu.HBM)


def on_device(
    hidden_in,
    frozen_query_matrix,
    factor_down,
    factor_up,
    query_gain,
    key_cache,
    value_cache,
    new_keys,
    new_values,
    cache_lengths,
):
    packed, own, lent = pl.pallas_call(
        pack_factors,
        out_shape=(
            jax.ShapeDtypeStruct((8, 16, 384), bf16),
            pltpu.VMEM((4, 8 * 384), bf16),
            jax.ShapeDtypeStruct((4, 8 * 384), bf16),
        ),
        in_specs=hbm(3),
        out_specs=(hbm(1)[0], *whole(2)),
        scratch_shapes=[
            pltpu.VMEM((64, 320), bf16),
            pltpu.VMEM((4, 256), bf16),
            pltpu.VMEM((2, 2, 5120), bf16),
            pltpu.VMEM((16, 128), f32),
            pltpu.VMEM((16, 384), bf16),
            pltpu.VMEM((4, 5120), f32),
            pltpu.SemaphoreType.DMA((11,)),
        ],
        compiler_params=room,
        name="pack_factors",
    )(far(factor_down.T), far(factor_up), far(hidden_in))
    factors = exchange(packed, "z", z_order)
    other = lax.ppermute(lent, "ylo", ((0, 1), (1, 0)))
    terms, pick, put, keys, values = pl.pallas_call(
        project,
        out_shape=(
            jax.ShapeDtypeStruct((16, 256), f32),
            jax.ShapeDtypeStruct((32, 128), bf16),
            jax.ShapeDtypeStruct((48, 256), bf16),
            pltpu.VMEM(key_cache.shape, bf16),
            pltpu.VMEM(value_cache.shape, bf16),
        ),
        in_specs=hbm(4),
        out_specs=tuple(whole(5)),
        scratch_shapes=[
            pltpu.VMEM((2, 2, 5120), bf16),
            pltpu.VMEM((5120, 256), bf16),
            pltpu.SemaphoreType.DMA((4,)),
        ],
        compiler_params=room,
        cost_estimate=pl.CostEstimate(flops=2 * 4 * 5120 * 256, bytes_accessed=8 * 2**20, transcendentals=0),
        name="project",
    )(far(hidden_in), far(frozen_query_matrix), far(key_cache), far(value_cache))
    sent = pl.pallas_call(
        pack_queries,
        out_shape=jax.ShapeDtypeStruct((8, 48, 256), bf16),
        in_specs=whole(6),
        out_specs=whole(1)[0],
        scratch_shapes=[pltpu.VMEM((16, 8 * 384), bf16), pltpu.VMEM((128, 256), bf16)],
        compiler_params=room,
        name="pack_queries",
    )(own, other, terms, pick, put, factors)
    parts = exchange(sent, ("fsdp", "ylo"), y_order)
    partial = pl.pallas_call(
        attend,
        out_shape=jax.ShapeDtypeStruct((4, 24, 128), f32),
        in_specs=whole(7),
        out_specs=whole(1)[0],
        scratch_shapes=[pltpu.VMEM((32, 128), f32)] + [pltpu.VMEM((16, 128), f32)] * 2,
        compiler_params=room,
        name="attend",
    )(parts, query_gain.reshape(1, 128), keys, values, new_keys, new_values, cache_lengths.reshape(1, 2))
    partial = exchange(partial, "fsdp", fsdp_order)
    return pl.pallas_call(
        merge,
        out_shape=jax.ShapeDtypeStruct((2, 2, 256), bf16),
        in_specs=whole(1),
        out_specs=whole(1)[0],
        compiler_params=room,
        name="merge",
    )(partial)


def solution(mesh):
    rep = ("z", "ylo")
    lines = mesh.devices.reshape(mesh.devices.shape[0] // 2, 2, *mesh.devices.shape[1:])
    lines = jax.sharding.Mesh(lines, rep + mesh.axis_names[1:])
    placed = (
        P(rep, None, None),
        P(None, ("tp", "fsdp")),
        P(rep, None),
        P(rep, ("tp", "fsdp")),
        P(),
        P(rep, "fsdp", "tp"),
        P(rep, "fsdp", "tp"),
        P(rep, None, "tp"),
        P(rep, None, "tp"),
        P(rep),
    )
    return jax.shard_map(
        on_device,
        mesh=lines,
        in_specs=placed,
        out_specs=P(rep, None, ("tp", "fsdp")),
        check_vma=False,
    )
```
